128 devices in a mesh: replica: 8 (over x_hi, y), fsdp: 16 (over z, x_lo, core).
Axes of the slice: x: 4 (x_hi: 2, x_lo: 2; x = x_hi * 2 + x_lo), y: 4, z: 4, core: 2. Of those that a mesh axis runs over, the one named last changes fastest.
Arguments:
- local_weights: float32 [8, 16384, 2048], P('replica', 'fsdp'), may hold values from -25 to 25
- anchor: bfloat16 [16384, 2048], P('fsdp'), may hold values from -5 to 5
- outer_weights: float32 [16384, 2048], P('replica', 'fsdp'), may hold values from -5 to 5
- momentum: float32 [16384, 2048], P('replica', 'fsdp'), may hold values from -0.6 to 0.6
Outputs:
- new_outer: float32 [16384, 2048], P('replica', 'fsdp')
- new_momentum: float32 [16384, 2048], P('replica', 'fsdp')
- blended: float32 [8, 16384, 2048], P('replica', 'fsdp')
The draws below stay inside these ranges and needn't reach their ends.
All inputs are finite; a program needn't handle non-finite values.
Results may differ from the reference program's by a relative error of at most 0.0049.
Values may be sent and summed in bfloat16 or wider, within the bound.
A program may use at most 128 MiB of HBM per device.

```python
import jax
import jax.numpy as jnp
from jax import lax

QB = 128
C = 2048
ROWS = 16384
REPLICAS = 8


def shared_base(key):
    normal_base = jax.random.normal(jax.random.fold_in(key, 100), (ROWS, C), jnp.float32)
    return jnp.clip(normal_base, -4.5, 4.5)


def draw_outer_weights(key, part):
    base_rows = shared_base(key)
    key = jax.random.fold_in(key, 7)
    own_noise = jnp.clip(0.25 * jax.random.normal(key, (ROWS, C), jnp.float32), -0.5, 0.5)
    return base_rows + own_noise


def draw_anchor(key, part):
    base_rows = shared_base(key)
    key = jax.random.fold_in(key, 5)
    own_noise = jnp.clip(0.3 * jax.random.normal(key, (ROWS, C), jnp.float32), -0.5, 0.5)
    return (base_rows + own_noise).astype(jnp.bfloat16)


def draw_local_weights(key, part):
    base_rows = shared_base(key)
    key = jax.random.fold_in(key, 3)
    key_rows, key_cols, key_own = jax.random.split(key, 3)
    row_factor = jnp.power(10.0, jax.random.uniform(key_rows, (ROWS, 1), jnp.float32) - 1.0)
    col_factor = jnp.power(10.0, jax.random.uniform(key_cols, (1, C), jnp.float32) - 1.0)
    ramp_rows = ((1.0 + 2.0 * jnp.arange(ROWS, dtype=jnp.float32) / (ROWS - 1)) / 3.0).reshape(ROWS, 1)
    noise_part = jnp.clip(jax.random.normal(key_own, (REPLICAS, ROWS, C), jnp.float32), -4.0, 4.0)
    amplitude = 5.0
    drift_part = amplitude * row_factor * col_factor * ramp_rows
    return base_rows[None] - drift_part[None] * noise_part


def block_levels(own_key, shape, pieces, low, top_value):
    def one(position, parts):
        draws = jax.random.uniform(jax.random.fold_in(jax.random.fold_in(own_key, 6), position), (parts,), jnp.float32, low / len(pieces), top_value / len(pieces))
        return jnp.repeat(jnp.exp(draws), shape[position] // parts).reshape((-1,) + (1,) * (len(shape) - position - 1))

    factor_of = one(*pieces[0])
    for cut in pieces[1:]:
        factor_of = factor_of * one(*cut)
    return factor_of


def noise(stream_key, shape, spread, most, shards=(), held_as=jnp.bfloat16):
    entries = spread * jax.random.normal(stream_key, shape, jnp.float32)
    if shards:
        entries = entries * block_levels(stream_key, shape, shards, -0.22, 0.18)
    return jnp.clip(entries, -most, most).astype(held_as)


def setup_inputs(seed: int = 0) -> dict:
    arg_keys = jax.random.split(jax.random.key(seed), 5)
    return {
        "local_weights": draw_local_weights(jax.random.fold_in(arg_keys[4], 71), 0),
        "anchor": draw_anchor(jax.random.fold_in(arg_keys[4], 71), 0),
        "outer_weights": draw_outer_weights(jax.random.fold_in(arg_keys[4], 71), 0),
        "momentum": noise(arg_keys[3], (ROWS, C), 0.1, 0.6, ((0, 8), (1, 16)), jnp.float32),
    }


CLIP_RMS = 0.1
OUTER_RATE = 0.7
MOMENTUM_RATE = 0.9
LEVELS = 127.0

def dequantized_replica(anchor_wide, local_rows):
    pseudo = anchor_wide - local_rows
    grouped = pseudo.reshape(ROWS, C // QB, QB)
    scales_half = ((lax.optimization_barrier(jnp.max(jnp.abs(grouped), axis=2, keepdims=True)) + 1e-06) / LEVELS).astype(jnp.bfloat16)
    scales_wide = lax.optimization_barrier(scales_half).astype(jnp.float32)
    quantized = jnp.floor(grouped / scales_wide + 0.5).astype(jnp.bfloat16)
    return (quantized.astype(jnp.float32) * scales_wide).reshape(ROWS, C)

def reference(local_weights, anchor, outer_weights, momentum):
    anchor_wide = anchor.astype(jnp.float32)

    def accumulate(running, local_rows):
        return (running + dequantized_replica(anchor_wide, local_rows), None)
    summed, unused = lax.scan(accumulate, jnp.zeros((ROWS, C), jnp.float32), local_weights)
    average = summed / REPLICAS
    mean_square = jnp.mean(average * average)
    factor = jnp.minimum(1.0, CLIP_RMS / jnp.sqrt(mean_square + 1e-06))
    clipped = average * factor
    new_momentum = MOMENTUM_RATE * momentum + clipped
    new_outer = outer_weights - OUTER_RATE * (clipped + MOMENTUM_RATE * new_momentum)
    outer_half = new_outer.astype(jnp.bfloat16)
    outer_back = lax.optimization_barrier(outer_half).astype(jnp.float32)
    blended = 0.5 * local_weights + 0.5 * outer_back[None]
    return (new_outer, new_momentum, blended)
```

```python
import jax
import jax.numpy as jnp
from jax import lax
from jax.experimental import pallas as pl
from jax.experimental.pallas import tpu as pltpu
from jax.sharding import PartitionSpec as P

MESH = pl.DeviceIdType.MESH
BF16 = jnp.bfloat16
F32 = jnp.float32

QB = 128
CLIP_RMS = 0.1
OUTER_RATE = 0.7
MOMENTUM_RATE = 0.9
LEVELS = 127.0

NR = 8
NF = 16
PIECE = 128
HALF = 64
QUARTER = 32
LOOKAHEAD = 4


def kernel(
    loc_h, anc_h, ow_h, mo_h,
    no_h, nm_h, bl_h,
    loc, anc, dq, ra, relb, finb, rela, fina, xb, tot, toth, g,
    u, w, ow, mo, oh, t, obuf, part, s1, part2, s2,
    ld, iosem, osem, ss, rs, zs_sem, zr_sem, ps_sem, pr_sem, as_sem, ar_sem,
):
    rows, width = dq.shape
    r = lax.axis_index("replica")
    f = lax.axis_index("fsdp")
    xh, y = r // 4, r % 4
    z, xl, c = f // 4, (f // 2) % 2, f % 2
    plane = r * 4 + xl * 2 + c
    yl, yr, yo = (y + 3) % 4, (y + 1) % 4, (y + 2) % 4
    left = (xh * 4 + yl, f)
    right = (xh * 4 + yr, f)
    across = ((1 - xh) * 4 + y, f)

    def row(x_of, y_of, side, offset=0):
        return pl.multiple_of((4 * x_of + y_of) * PIECE + side * HALF + offset, QUARTER)

    barrier = pltpu.get_barrier_semaphore()

    def greet_plane(i, _):
        other = (plane + i) % 32
        pl.semaphore_signal(
            barrier, inc=1, device_id=(other // 4, z * 4 + other % 4), device_id_type=MESH
        )
        return 0

    lax.fori_loop(1, 32, greet_plane, 0)
    for dz in (1, 2, 3):
        pl.semaphore_signal(
            barrier, inc=1, device_id=(r, ((z + dz) % 4) * 4 + xl * 2 + c), device_id_type=MESH
        )

    far = 1 - xh
    units = [
        (far, yo, 1), (far, yo, 0), (far, yr, 1), (far, yl, 1), (far, yr, 0), (xh, yo, 1),
        (far, yl, 0), (xh, yr, 1), (xh, yl, 1), (far, y, 0), (far, y, 1), (xh, yo, 0),
        (xh, yr, 0), (xh, yl, 0), (xh, y, 1), (xh, y, 0),
    ]
    loads = []
    for k, unit in enumerate(units):
        at = pl.ds(row(*unit), HALF)
        loads.append(
            (
                pltpu.make_async_copy(loc_h.at[0, at], loc.at[at], ld.at[2 * k]),
                pltpu.make_async_copy(anc_h.at[at], anc.at[at], ld.at[2 * k + 1]),
            )
        )
    state_in = (
        pltpu.make_async_copy(ow_h, ow, iosem.at[0]),
        pltpu.make_async_copy(mo_h, mo, iosem.at[1]),
    )

    def begin(k):
        for copy in loads[k]:
            copy.start()

    begin(0)
    for copy in state_in:
        copy.start()
    for k in range(1, LOOKAHEAD):
        begin(k)

    def quantize(k):
        for copy in loads[k]:
            copy.wait()
        if k + LOOKAHEAD < len(units):
            begin(k + LOOKAHEAD)
        base = row(*units[k])

        def step(i, _):
            at = pl.ds(pl.multiple_of(base + i * 16, 16), 16)
            pseudo = anc[at, :].astype(F32) - loc[at, :]
            done = []
            for b in range(width // QB):
                block = pseudo[:, b * QB : (b + 1) * QB]
                largest = jnp.max(jnp.abs(block), axis=1, keepdims=True)
                scale = ((largest + 1e-06) / LEVELS).astype(BF16).astype(F32)
                level = jnp.floor(block / scale + 0.5)
                done.append((level * scale).astype(BF16))
            dq[at, :] = jnp.concatenate(done, axis=1)
            return 0

        lax.fori_loop(0, HALF // 16, step, 0)

    def add(dst, dst_base, terms, count):
        def step(i, _):
            value = None
            for ref, base in terms:
                x = ref[pl.ds(pl.multiple_of(base + i * 16, 16), 16), :].astype(F32)
                value = x if value is None else value + x
            dst[pl.ds(pl.multiple_of(dst_base + i * 16, 16), 16), :] = value.astype(dst.dtype)
            return 0

        lax.fori_loop(0, count // 16, step, 0)

    sent = []

    def put(src, dst, device):
        k = len(sent)
        copy = pltpu.make_async_remote_copy(
            src_ref=src, dst_ref=dst, send_sem=ss.at[k], recv_sem=rs.at[k],
            device_id=device, device_id_type=MESH,
        )
        copy.start()
        sent.append(copy)
        return copy

    def prepare(i, _):
        at = pl.ds(pl.multiple_of(i * 128, 128), 128)
        oh[at, :] = (
            ow[at, :] - (OUTER_RATE * MOMENTUM_RATE * MOMENTUM_RATE) * mo[at, :]
        ).astype(BF16)
        return 0

    for copy in state_in:
        copy.wait()
    lax.fori_loop(0, 16, prepare, 0)
    quantize(0)
    pl.semaphore_wait(barrier, 34)

    sides = {"l": left, "r": right}
    fb = [far, xh]
    relb_copies, finb_copies = [[], []], [[], []]

    def send_relay_b(j):
        base = row(fb[j], yo, 1)
        relb_copies[j] = [
            put(dq.at[pl.ds(base, QUARTER)], relb.at[pl.ds(j * 64, QUARTER)], right),
            put(dq.at[pl.ds(base + QUARTER, QUARTER)], relb.at[pl.ds(j * 64 + QUARTER, QUARTER)], left),
        ]

    def send_now(src_base, dst, dst_base, side, offset):
        return put(
            dq.at[pl.ds(src_base + offset, QUARTER)],
            dst.at[pl.ds(dst_base + offset, QUARTER)],
            sides[side],
        )

    ra_copies = []

    def send_a(i, y_of):
        ra_copies.append(put(dq.at[pl.ds(row(far, y_of, 0), HALF)], ra.at[pl.ds(i * HALF, HALF)], across))

    send_relay_b(0)

    def spread(b, _):
        c_of, p = b // 8, b % 8
        src = oh.at[pl.ds(pl.multiple_of(b * 128, 128), 128)]
        dst = t.at[
            pl.ds(pl.multiple_of((r // 2) * 128, 128), 128),
            pl.ds(pl.multiple_of((2 * xl + c) * 128, 128), 128),
        ]
        own = jnp.logical_and(jnp.logical_and(p == r, y % 2 == xl), c_of == c)

        @pl.when(own)
        def _():
            pltpu.make_async_copy(src, dst, pr_sem.at[0]).start()

        @pl.when(jnp.logical_not(own))
        def _():
            pltpu.make_async_remote_copy(
                src_ref=src, dst_ref=dst, send_sem=ps_sem.at[0], recv_sem=pr_sem.at[0],
                device_id=(p, z * 4 + (y % 2) * 2 + c_of), device_id_type=MESH,
            ).start()

        return 0

    lax.fori_loop(0, 16, spread, 0)

    quantize(1)
    send_a(0, yo)
    quantize(2)
    finb_copies[0].append(send_now(row(far, yr, 1), finb, 0, "r", QUARTER))
    quantize(3)
    finb_copies[0].append(send_now(row(far, yl, 1), finb, HALF, "l", 0))
    quantize(4)
    send_a(1, yr)
    quantize(5)
    send_relay_b(1)
    quantize(6)
    send_a(2, yl)

    def relay_b(j):
        for copy in relb_copies[j]:
            copy.wait_recv()
        base = row(fb[j], yr, 1)
        add(dq, base, ((dq, base), (relb, j * 64)), QUARTER)
        finb_copies[j].append(send_now(base, finb, j * 128, "r", 0))
        base = row(fb[j], yl, 1) + QUARTER
        add(dq, base, ((dq, base), (relb, j * 64 + QUARTER)), QUARTER)
        finb_copies[j].append(send_now(base - QUARTER, finb, j * 128 + HALF, "l", QUARTER))

    quantize(7)
    finb_copies[1].append(send_now(row(xh, yr, 1), finb, 128, "r", QUARTER))
    quantize(8)
    finb_copies[1].append(send_now(row(xh, yl, 1), finb, 128 + HALF, "l", 0))
    relay_b(0)
    quantize(9)
    send_a(3, y)
    quantize(10)
    quantize(11)

    def pair(i, y_of):
        ra_copies[i].wait_recv()
        base = row(xh, y_of, 0)
        add(dq, base, ((dq, base), (ra, i * HALF)), HALF)
        return base

    base = pair(0, yo)
    rela_copies = [
        put(dq.at[pl.ds(base, QUARTER)], rela.at[pl.ds(0, QUARTER)], right),
        put(dq.at[pl.ds(base + QUARTER, QUARTER)], rela.at[pl.ds(QUARTER, QUARTER)], left),
    ]
    quantize(12)
    quantize(13)
    relay_b(1)
    quantize(14)
    quantize(15)

    for copy in finb_copies[0]:
        copy.wait_recv()
    base = row(far, y, 1)
    add(dq, base, ((dq, base), (finb, 0), (finb, HALF)), HALF)
    xb_copy = put(dq.at[pl.ds(base, HALF)], xb, across)

    pltpu.make_async_copy(t, t, pr_sem.at[0]).wait()

    def along_z(src_of, dst_of, q):
        for dz in (1, 2, 3):
            z_of = (z + dz) % 4
            pltpu.make_async_remote_copy(
                src_ref=src_of(z_of), dst_ref=dst_of(z), send_sem=zs_sem.at[q], recv_sem=zr_sem.at[q],
                device_id=(r, z_of * 4 + xl * 2 + c), device_id_type=MESH,
            ).start()
        pltpu.make_async_copy(src_of(z), dst_of(z), zr_sem.at[q]).start()

    along_z(
        lambda z_of: t.at[pl.ds(pl.multiple_of(z_of * 128, 128), 128)],
        lambda z_of: obuf.at[:, pl.ds(pl.multiple_of(z_of * 512, 512), 512)],
        0,
    )

    base = pair(1, yr)
    fina_copies = [send_now(base, fina, 0, "r", QUARTER)]
    base = pair(2, yl)
    fina_copies.append(send_now(base, fina, HALF, "l", 0))
    for copy in rela_copies:
        copy.wait_recv()
    base = row(xh, yr, 0)
    add(dq, base, ((dq, base), (rela, 0)), QUARTER)
    fina_copies.append(send_now(base, fina, 0, "r", 0))
    base = row(xh, yl, 0) + QUARTER
    add(dq, base, ((dq, base), (rela, QUARTER)), QUARTER)
    fina_copies.append(send_now(base - QUARTER, fina, HALF, "l", QUARTER))

    def total(tot_base, terms, carry):
        def step(i, carry):
            value = None
            for ref, base in terms:
                x = ref[pl.ds(pl.multiple_of(base + i * 16, 16), 16), :].astype(F32)
                value = x if value is None else value + x
            at = pl.ds(pl.multiple_of(tot_base + i * 16, 16), 16)
            tot[at, :] = value
            toth[at, :] = value.astype(BF16)
            square = value * value
            for a in range(0, 16, 8):
                for b in range(0, width, 128):
                    carry = carry + square[a : a + 8, b : b + 128]
            return carry

        return lax.fori_loop(0, HALF // 16, step, carry)

    for copy in finb_copies[1]:
        copy.wait_recv()
    xb_copy.wait_recv()
    carry = total(
        HALF,
        ((dq, row(xh, y, 1)), (finb, 128), (finb, 128 + HALF), (xb, 0)),
        jnp.zeros((8, 128), F32),
    )
    ra_copies[3].wait_recv()
    for copy in fina_copies:
        copy.wait_recv()
    carry = total(
        0, ((dq, row(xh, y, 0)), (ra, 3 * HALF), (fina, 0), (fina, HALF)), carry
    )

    part[...] = carry
    s1[pl.ds(pl.multiple_of(plane * 8, 8), 8), :] = carry

    def tell_plane(i, _):
        other = (plane + i) % 32
        pltpu.make_async_remote_copy(
            src_ref=part, dst_ref=s1.at[pl.ds(pl.multiple_of(plane * 8, 8), 8)],
            send_sem=as_sem.at[0], recv_sem=ar_sem.at[0],
            device_id=(other // 4, z * 4 + other % 4), device_id_type=MESH,
        ).start()
        return 0

    lax.fori_loop(1, 32, tell_plane, 0)

    along_z(
        lambda z_of: toth.at[:, pl.ds(pl.multiple_of(z_of * 512, 512), 512)],
        lambda z_of: u.at[pl.ds(pl.multiple_of(z_of * 128, 128), 128)],
        1,
    )

    def wait_bytes(ref, sem):
        pltpu.make_async_copy(ref, ref, sem).wait()

    wait_bytes(s1.at[pl.ds(0, 31 * 8)], ar_sem.at[0])
    wait_bytes(s1.at[pl.ds(0, 31 * 8)], as_sem.at[0])
    in_plane = s1[0:8, :]
    for k in range(1, 32):
        in_plane = in_plane + s1[8 * k : 8 * k + 8, :]
    part2[...] = in_plane
    s2[pl.ds(pl.multiple_of(z * 8, 8), 8), :] = in_plane
    for dz in (1, 2, 3):
        z_of = (z + dz) % 4
        pltpu.make_async_remote_copy(
            src_ref=part2, dst_ref=s2.at[pl.ds(pl.multiple_of(z * 8, 8), 8)],
            send_sem=as_sem.at[1], recv_sem=ar_sem.at[1],
            device_id=(r, z_of * 4 + xl * 2 + c), device_id_type=MESH,
        ).start()
    wait_bytes(obuf, zr_sem.at[0])
    wait_bytes(s2.at[pl.ds(0, 24)], ar_sem.at[1])
    wait_bytes(s2.at[pl.ds(0, 24)], as_sem.at[1])
    everywhere = s2[0:8, :] + s2[8:16, :] + s2[16:24, :] + s2[24:32, :]
    squares = jnp.sum(everywhere, keepdims=True)
    entries = float(rows * NF) * width
    mean = squares * (1.0 / (NR * NR * entries))
    factor = jnp.minimum(1.0, CLIP_RMS / jnp.sqrt(mean + 1e-06)) * (1.0 / NR)
    weight = (OUTER_RATE * (1.0 + MOMENTUM_RATE)) * factor

    own = r * PIECE

    def outer_half(base):
        def step(i, _):
            at = pl.ds(pl.multiple_of(base + i * 16, 16), 16)
            g[pl.ds(pl.multiple_of(own + base + i * 16, 16), 16), :] = (
                obuf[at, :].astype(F32) - weight * tot[at, :]
            ).astype(BF16)
            return 0

        lax.fori_loop(0, HALF // 16, step, 0)

    def move(base, count, device):
        at = pl.ds(pl.multiple_of(base, QUARTER), count)
        return put(g.at[at], g.at[at], device)

    def ring(base):
        r0 = move(base, QUARTER, right)
        l1 = move(base + QUARTER, QUARTER, left)
        r1 = move(base + QUARTER, QUARTER, right)
        l0 = move(base, QUARTER, left)
        return r0, l1, r1, l0

    def pass_on(x_of, side, copies):
        r0, l1 = copies[:2]
        r0.wait_recv()
        first = move(row(x_of, yl, side), QUARTER, right)
        l1.wait_recv()
        second = move(row(x_of, yr, side) + QUARTER, QUARTER, left)
        return first, second

    outer_half(HALF)
    over_b = move(row(xh, y, 1), HALF, across)
    outer_half(0)
    ring_a = ring(row(xh, y, 0))
    over_a = [move(row(xh, y, 0), HALF, across)]
    ring_b = ring(row(xh, y, 1))

    wait_bytes(u, zr_sem.at[1])

    def to_owner(b, _):
        z_of, k = b // 4, b % 4
        src = u.at[
            pl.ds(pl.multiple_of(z_of * 128, 128), 128), pl.ds(pl.multiple_of(k * 128, 128), 128)
        ]
        dst = w.at[pl.ds(pl.multiple_of(c * 1024 + r * 128, 128), 128)]
        is_own = jnp.logical_and(2 * z_of + xl == r, k == 2 * xl + c)

        @pl.when(is_own)
        def _():
            pltpu.make_async_copy(src, dst, pr_sem.at[1]).start()

        @pl.when(jnp.logical_not(is_own))
        def _():
            pltpu.make_async_remote_copy(
                src_ref=src, dst_ref=dst, send_sem=ps_sem.at[1], recv_sem=pr_sem.at[1],
                device_id=(2 * z_of + xl, z * 4 + k), device_id_type=MESH,
            ).start()

        return 0

    lax.fori_loop(0, 16, to_owner, 0)

    def blend(base):
        def step(i, _):
            at = pl.ds(pl.multiple_of(base + i * 16, 16), 16)
            loc[at, :] = 0.5 * loc[at, :] + 0.5 * g[at, :].astype(F32)
            return 0

        lax.fori_loop(0, HALF // 16, step, 0)
        at = pl.ds(base, HALF)
        pltpu.make_async_copy(loc.at[at], bl_h.at[0, at], osem.at[2]).start()

    blend(row(xh, y, 1))
    blend(row(xh, y, 0))
    on_a = pass_on(xh, 0, ring_a)
    ring_a[2].wait_recv()
    over_a.append(move(row(xh, yl, 0), HALF, across))
    ring_a[3].wait_recv()
    over_a.append(move(row(xh, yr, 0), HALF, across))
    blend(row(xh, yl, 0))
    blend(row(xh, yr, 0))
    over_b.wait_recv()
    ring_x = ring(row(far, y, 1))
    blend(row(far, y, 1))
    on_b = pass_on(xh, 1, ring_b)
    for copy in on_a:
        copy.wait_recv()
    over_a.append(move(row(xh, yo, 0), HALF, across))
    blend(row(xh, yo, 0))
    for copy in ring_b[2:]:
        copy.wait_recv()
    blend(row(xh, yl, 1))
    blend(row(xh, yr, 1))

    wait_bytes(w, pr_sem.at[1])

    def finish(i, _):
        at = pl.ds(pl.multiple_of(i * 128, 128), 128)
        clipped = factor * w[at, :].astype(F32)
        momentum = MOMENTUM_RATE * mo[at, :] + clipped
        ow[at, :] = ow[at, :] - OUTER_RATE * (clipped + MOMENTUM_RATE * momentum)
        mo[at, :] = momentum
        return 0

    lax.fori_loop(0, 16, finish, 0)
    state_out = (
        pltpu.make_async_copy(ow, no_h, osem.at[0]),
        pltpu.make_async_copy(mo, nm_h, osem.at[1]),
    )
    for copy in state_out:
        copy.start()

    over_a[0].wait_recv()
    blend(row(far, y, 0))
    on_x = pass_on(far, 1, ring_x)
    for copy in on_b:
        copy.wait_recv()
    blend(row(xh, yo, 1))
    for copy in ring_x[2:]:
        copy.wait_recv()
    blend(row(far, yl, 1))
    blend(row(far, yr, 1))
    over_a[1].wait_recv()
    blend(row(far, yl, 0))
    over_a[2].wait_recv()
    blend(row(far, yr, 0))
    for copy in on_x:
        copy.wait_recv()
    blend(row(far, yo, 1))
    over_a[3].wait_recv()
    blend(row(far, yo, 0))

    for copy in sent:
        copy.wait_send()
    wait_bytes(t.at[pl.ds(0, 384)], zs_sem.at[0])
    wait_bytes(u.at[pl.ds(0, 384)], zs_sem.at[1])
    in_place = y % 2 == xl
    for q, ref in ((0, t), (1, u)):

        @pl.when(in_place)
        def _():
            wait_bytes(ref.at[pl.ds(0, 480)], ps_sem.at[q])

        @pl.when(jnp.logical_not(in_place))
        def _():
            wait_bytes(ref, ps_sem.at[q])

    for copy in state_out:
        copy.wait()
    pltpu.make_async_copy(loc, bl_h.at[0], osem.at[2]).wait()


def on_device(local_weights, anchor, outer_weights, momentum):
    _, rows, width = local_weights.shape
    owned, tile = outer_weights.shape
    whole = pl.BlockSpec(memory_space=pl.ANY)
    vmem = pltpu.VMEM
    dma = pltpu.SemaphoreType.DMA
    return pl.pallas_call(
        kernel,
        out_shape=(
            jax.ShapeDtypeStruct((owned, tile), F32),
            jax.ShapeDtypeStruct((owned, tile), F32),
            jax.ShapeDtypeStruct((1, rows, width), F32),
        ),
        in_specs=[whole] * 4,
        out_specs=(whole,) * 3,
        scratch_shapes=[
            vmem((rows, width), F32),
            vmem((rows, width), BF16),
            vmem((rows, width), BF16),
            vmem((4 * HALF, width), BF16),
            vmem((128, width), BF16),
            vmem((256, width), BF16),
            vmem((64, width), BF16),
            vmem((128, width), BF16),
            vmem((HALF, width), BF16),
            vmem((PIECE, width), F32),
            vmem((PIECE, width), BF16),
            vmem((rows, width), BF16),
            vmem((512, 512), BF16),
            vmem((owned, tile), BF16),
            vmem((owned, tile), F32),
            vmem((owned, tile), F32),
            vmem((owned, tile), BF16),
            vmem((512, 512), BF16),
            vmem((PIECE, width), BF16),
            vmem((8, 128), F32),
            vmem((256, 128), F32),
            vmem((8, 128), F32),
            vmem((32, 128), F32),
            dma((32,)),
            dma((2,)),
            dma((3,)),
            dma((64,)),
            dma((64,)),
            dma((2,)),
            dma((2,)),
            dma((2,)),
            dma((2,)),
            dma((2,)),
            dma((2,)),
        ],
        compiler_params=pltpu.CompilerParams(
            collective_id=0, has_side_effects=True, vmem_limit_bytes=56 << 20
        ),
    )(local_weights, anchor, outer_weights, momentum)


def solution(mesh):
    placed = (
        P("replica", "fsdp", None),
        P("fsdp", None),
        P("replica", "fsdp"),
        P("replica", "fsdp"),
    )
    return jax.shard_map(
        on_device,
        mesh=mesh,
        in_specs=placed,
        out_specs=(P("replica", "fsdp"), P("replica", "fsdp"), P("replica", "fsdp", None)),
        check_vma=False,
    )
```

```python
import jax
import jax.numpy as jnp
from jax import lax
from jax.experimental import pallas as pl
from jax.experimental.pallas import tpu as pltpu
from jax.sharding import PartitionSpec as P

MESH = pl.DeviceIdType.MESH
BF16 = jnp.bfloat16
F32 = jnp.float32

QB = 128
CLIP_RMS = 0.1
OUTER_RATE = 0.7
MOMENTUM_RATE = 0.9
LEVELS = 127.0

NR = 8
NF = 16
PIECE = 128
HALF = 64
QUARTER = 32
LOOKAHEAD = 4


def kernel(
    loc_h, anc_h, ow_h, mo_h,
    ow, mo, blended,
    anc, dq, ra, relb, finb, rela, fina, xb, tot, toth, g,
    u, w, oh, v, t, obuf, part, s1, part2, s2,
    ld, iosem, ss, rs, zs_sem, zr_sem, ps_sem, pr_sem, as_sem, ar_sem,
):
    rows, width = dq.shape
    loc = blended.at[0]
    r = lax.axis_index("replica")
    f = lax.axis_index("fsdp")
    xh, y = r // 4, r % 4
    z, xl, c = f // 4, (f // 2) % 2, f % 2
    plane = r * 4 + xl * 2 + c
    chip = r * 2 + xl
    column = z * 2 + c
    yl, yr, yo = (y + 3) % 4, (y + 1) % 4, (y + 2) % 4
    left = (xh * 4 + yl, f)
    right = (xh * 4 + yr, f)
    across = ((1 - xh) * 4 + y, f)

    def row(x_of, y_of, side, offset=0):
        return pl.multiple_of((4 * x_of + y_of) * PIECE + side * HALF + offset, QUARTER)

    far = 1 - xh
    units = [
        (far, yo, 1), (far, yo, 0), (far, yr, 1), (far, yl, 1), (far, yr, 0), (xh, yo, 1),
        (far, yl, 0), (xh, yr, 1), (xh, yl, 1), (far, y, 0), (far, y, 1), (xh, yo, 0),
        (xh, yr, 0), (xh, yl, 0), (xh, y, 1), (xh, y, 0),
    ]
    loads = []
    for k, unit in enumerate(units):
        at = pl.ds(row(*unit), HALF)
        loads.append(
            (
                pltpu.make_async_copy(loc_h.at[0, at], loc.at[at], ld.at[2 * k]),
                pltpu.make_async_copy(anc_h.at[at], anc.at[at], ld.at[2 * k + 1]),
            )
        )
    state_in = (
        pltpu.make_async_copy(ow_h, ow, iosem.at[0]),
        pltpu.make_async_copy(mo_h, mo, iosem.at[1]),
    )

    def begin(k):
        for copy in loads[k]:
            copy.start()

    begin(0)
    for copy in state_in:
        copy.start()
    for k in range(1, LOOKAHEAD):
        begin(k)

    barrier = pltpu.get_barrier_semaphore()

    def greet_plane(i, _):
        other = (plane + i) % 32
        pl.semaphore_signal(
            barrier, inc=1, device_id=(other // 4, z * 4 + other % 4), device_id_type=MESH
        )
        return 0

    lax.fori_loop(1, 32, greet_plane, 0)
    for dz in (1, 2, 3):
        for c_of in (0, 1):
            pl.semaphore_signal(
                barrier, inc=1, device_id=(r, ((z + dz) % 4) * 4 + xl * 2 + c_of), device_id_type=MESH
            )

    def quantize(k):
        for copy in loads[k]:
            copy.wait()
        if k + LOOKAHEAD < len(units):
            begin(k + LOOKAHEAD)
        base = row(*units[k])

        def step(i, _):
            at = pl.ds(pl.multiple_of(base + i * 16, 16), 16)
            pseudo = anc[at, :].astype(F32) - loc[at, :]
            done = []
            for b in range(width // QB):
                block = pseudo[:, b * QB : (b + 1) * QB]
                largest = jnp.max(jnp.abs(block), axis=1, keepdims=True)
                scale = ((largest + 1e-06) / LEVELS).astype(BF16).astype(F32)
                level = jnp.floor(block / scale + 0.5)
                done.append((level * scale).astype(BF16))
            dq[at, :] = jnp.concatenate(done, axis=1)
            return 0

        lax.fori_loop(0, HALF // 16, step, 0)

    def add(dst, dst_base, terms, count):
        def step(i, _):
            value = None
            for ref, base in terms:
                x = ref[pl.ds(pl.multiple_of(base + i * 16, 16), 16), :].astype(F32)
                value = x if value is None else value + x
            dst[pl.ds(pl.multiple_of(dst_base + i * 16, 16), 16), :] = value.astype(dst.dtype)
            return 0

        lax.fori_loop(0, count // 16, step, 0)

    sent = []

    def put(src, dst, device):
        k = len(sent)
        copy = pltpu.make_async_remote_copy(
            src_ref=src, dst_ref=dst, send_sem=ss.at[k], recv_sem=rs.at[k],
            device_id=device, device_id_type=MESH,
        )
        copy.start()
        sent.append(copy)
        return copy

    def prepare(i, _):
        at = pl.ds(pl.multiple_of(i * 128, 128), 128)
        oh[i // 8, i % 4, (i // 4) % 2] = (
            ow[at, :] - (OUTER_RATE * MOMENTUM_RATE * MOMENTUM_RATE) * mo[at, :]
        ).astype(BF16)
        return 0

    for copy in state_in:
        copy.wait()
    lax.fori_loop(0, 16, prepare, 0)
    quantize(0)
    pl.semaphore_wait(barrier, 37)

    sides = {"l": left, "r": right}
    fb = [far, xh]
    relb_copies, finb_copies = [[], []], [[], []]

    def send_relay_b(j):
        base = row(fb[j], yo, 1)
        relb_copies[j] = [
            put(dq.at[pl.ds(base, QUARTER)], relb.at[pl.ds(j * 64, QUARTER)], right),
            put(dq.at[pl.ds(base + QUARTER, QUARTER)], relb.at[pl.ds(j * 64 + QUARTER, QUARTER)], left),
        ]

    def send_now(src_base, dst, dst_base, side, offset):
        return put(
            dq.at[pl.ds(src_base + offset, QUARTER)],
            dst.at[pl.ds(dst_base + offset, QUARTER)],
            sides[side],
        )

    ra_copies = []

    def send_a(i, y_of):
        ra_copies.append(put(dq.at[pl.ds(row(far, y_of, 0), HALF)], ra.at[pl.ds(i * HALF, HALF)], across))

    send_relay_b(0)

    def share(src, dst, q, own, device):
        @pl.when(own)
        def _():
            pltpu.make_async_copy(src, dst, pr_sem.at[q]).start()

        @pl.when(jnp.logical_not(own))
        def _():
            pltpu.make_async_remote_copy(
                src_ref=src, dst_ref=dst, send_sem=ps_sem.at[q], recv_sem=pr_sem.at[q],
                device_id=device, device_id_type=MESH,
            ).start()

    def spread_y(b):
        c_of, y_of = b // 4, b % 4
        share(
            oh.at[c_of, y_of], v.at[y, :, c], 0,
            jnp.logical_and(y_of == y, c_of == c), (xh * 4 + y_of, z * 4 + xl * 2 + c_of),
        )

    def spread_x(b):
        x_of, y_of = b // 4, b % 4
        dst = t.at[2 * xh + y_of // 2, xl]
        share(
            v.at[y_of, x_of], dst, 2,
            jnp.logical_and(x_of == xh, y_of % 2 == xl), (x_of * 4 + y, z * 4 + (y_of % 2) * 2 + c),
        )

    for b in range(8):
        spread_y(b)

    quantize(1)
    send_a(0, yo)
    quantize(2)
    finb_copies[0].append(send_now(row(far, yr, 1), finb, 0, "r", QUARTER))
    quantize(3)
    finb_copies[0].append(send_now(row(far, yl, 1), finb, HALF, "l", 0))
    quantize(4)
    send_a(1, yr)
    quantize(5)
    send_relay_b(1)
    quantize(6)
    send_a(2, yl)

    def relay_b(j):
        for copy in relb_copies[j]:
            copy.wait_recv()
        base = row(fb[j], yr, 1)
        add(dq, base, ((dq, base), (relb, j * 64)), QUARTER)
        finb_copies[j].append(send_now(base, finb, j * 128, "r", 0))
        base = row(fb[j], yl, 1) + QUARTER
        add(dq, base, ((dq, base), (relb, j * 64 + QUARTER)), QUARTER)
        finb_copies[j].append(send_now(base - QUARTER, finb, j * 128 + HALF, "l", QUARTER))

    quantize(7)
    finb_copies[1].append(send_now(row(xh, yr, 1), finb, 128, "r", QUARTER))
    quantize(8)
    finb_copies[1].append(send_now(row(xh, yl, 1), finb, 128 + HALF, "l", 0))
    pltpu.make_async_copy(v, v, pr_sem.at[0]).wait()
    for b in range(8):
        spread_x(b)
    relay_b(0)
    quantize(9)
    send_a(3, y)
    quantize(10)
    quantize(11)

    def pair(i, y_of):
        ra_copies[i].wait_recv()
        base = row(xh, y_of, 0)
        add(dq, base, ((dq, base), (ra, i * HALF)), HALF)
        return base

    base = pair(0, yo)
    rela_copies = [
        put(dq.at[pl.ds(base, QUARTER)], rela.at[pl.ds(0, QUARTER)], right),
        put(dq.at[pl.ds(base + QUARTER, QUARTER)], rela.at[pl.ds(QUARTER, QUARTER)], left),
    ]
    quantize(12)
    quantize(13)
    relay_b(1)
    quantize(14)
    quantize(15)

    for copy in finb_copies[0]:
        copy.wait_recv()
    base = row(far, y, 1)
    add(dq, base, ((dq, base), (finb, 0), (finb, HALF)), HALF)
    xb_copy = put(dq.at[pl.ds(base, HALF)], xb, across)

    pltpu.make_async_copy(t, t, pr_sem.at[2]).wait()

    def along_z(src_of, dst_of, q):
        for dz in (1, 2, 3):
            z_of = (z + dz) % 4
            pltpu.make_async_remote_copy(
                src_ref=src_of(z_of), dst_ref=dst_of(z), send_sem=zs_sem.at[q], recv_sem=zr_sem.at[q],
                device_id=(r, z_of * 4 + xl * 2 + c), device_id_type=MESH,
            ).start()
        pltpu.make_async_copy(src_of(z), dst_of(z), zr_sem.at[q]).start()

    along_z(
        lambda z_of: t.at[z_of],
        lambda z_of: obuf.at[z_of],
        0,
    )

    base = pair(1, yr)
    fina_copies = [send_now(base, fina, 0, "r", QUARTER)]
    base = pair(2, yl)
    fina_copies.append(send_now(base, fina, HALF, "l", 0))
    for copy in rela_copies:
        copy.wait_recv()
    base = row(xh, yr, 0)
    add(dq, base, ((dq, base), (rela, 0)), QUARTER)
    fina_copies.append(send_now(base, fina, 0, "r", 0))
    base = row(xh, yl, 0) + QUARTER
    add(dq, base, ((dq, base), (rela, QUARTER)), QUARTER)
    fina_copies.append(send_now(base - QUARTER, fina, HALF, "l", QUARTER))

    def total(tot_base, terms, carry):
        def step(i, carry):
            value = None
            for ref, base in terms:
                x = ref[pl.ds(pl.multiple_of(base + i * 16, 16), 16), :].astype(F32)
                value = x if value is None else value + x
            at = pl.ds(pl.multiple_of(tot_base + i * 16, 16), 16)
            tot[at, :] = value
            for b in range(width // 128):
                toth[pl.ds(pl.multiple_of(b * PIECE + tot_base + i * 16, 16), 16), :] = value[
                    :, b * 128 : (b + 1) * 128
                ].astype(BF16)
            square = value * value
            for a in range(0, 16, 8):
                for b in range(0, width, 128):
                    carry = carry + square[a : a + 8, b : b + 128]
            return carry

        return lax.fori_loop(0, HALF // 16, step, carry)

    for copy in finb_copies[1]:
        copy.wait_recv()
    xb_copy.wait_recv()
    carry = total(
        HALF,
        ((dq, row(xh, y, 1)), (finb, 128), (finb, 128 + HALF), (xb, 0)),
        jnp.zeros((8, 128), F32),
    )
    ra_copies[3].wait_recv()
    for copy in fina_copies:
        copy.wait_recv()
    carry = total(
        0, ((dq, row(xh, y, 0)), (ra, 3 * HALF), (fina, 0), (fina, HALF)), carry
    )

    part[...] = carry
    s1[pl.ds(pl.multiple_of(chip * 8, 8), 8), :] = carry

    def tell_plane(i, _):
        other = (chip + i) % 16
        pltpu.make_async_remote_copy(
            src_ref=part, dst_ref=s1.at[pl.ds(pl.multiple_of(chip * 8, 8), 8)],
            send_sem=as_sem.at[0], recv_sem=ar_sem.at[0],
            device_id=(other // 2, z * 4 + (other % 2) * 2 + c), device_id_type=MESH,
        ).start()
        return 0

    lax.fori_loop(1, 16, tell_plane, 0)

    along_z(
        lambda z_of: toth.at[pl.ds(pl.multiple_of(z_of * 512, 512), 512)],
        lambda z_of: u.at[pl.ds(pl.multiple_of(z_of * 512, 512), 512)],
        1,
    )

    def wait_bytes(ref, sem):
        pltpu.make_async_copy(ref, ref, sem).wait()

    wait_bytes(s1.at[pl.ds(0, 15 * 8)], ar_sem.at[0])
    wait_bytes(s1.at[pl.ds(0, 15 * 8)], as_sem.at[0])
    in_plane = s1[0:8, :]
    for k in range(1, 16):
        in_plane = in_plane + s1[8 * k : 8 * k + 8, :]
    part2[...] = in_plane
    s2[pl.ds(pl.multiple_of(column * 8, 8), 8), :] = in_plane
    for d in range(1, 8):
        other = (column + d) % 8
        pltpu.make_async_remote_copy(
            src_ref=part2, dst_ref=s2.at[pl.ds(pl.multiple_of(column * 8, 8), 8)],
            send_sem=as_sem.at[1], recv_sem=ar_sem.at[1],
            device_id=(r, (other // 2) * 4 + xl * 2 + other % 2), device_id_type=MESH,
        ).start()
    wait_bytes(obuf, zr_sem.at[0])
    wait_bytes(s2.at[pl.ds(0, 56)], ar_sem.at[1])
    wait_bytes(s2.at[pl.ds(0, 56)], as_sem.at[1])
    everywhere = s2[0:8, :]
    for k in range(1, 8):
        everywhere = everywhere + s2[8 * k : 8 * k + 8, :]
    squares = jnp.sum(everywhere, keepdims=True)
    entries = float(rows * NF) * width
    mean = squares * (1.0 / (NR * NR * entries))
    factor = jnp.minimum(1.0, CLIP_RMS / jnp.sqrt(mean + 1e-06)) * (1.0 / NR)
    weight = (OUTER_RATE * (1.0 + MOMENTUM_RATE)) * factor

    own = r * PIECE

    def outer_half(base):
        def step(i, _):
            at = pl.ds(pl.multiple_of(base + i * 16, 16), 16)
            to = pl.ds(pl.multiple_of(own + base + i * 16, 16), 16)
            for b in range(width // 128):
                cols = pl.ds(b * 128, 128)
                state = obuf[b // 4, (b // 2) % 2, b % 2, at, :]
                g[to, cols] = (state.astype(F32) - weight * tot[at, cols]).astype(BF16)
            return 0

        lax.fori_loop(0, HALF // 16, step, 0)

    def move(base, count, device):
        at = pl.ds(pl.multiple_of(base, QUARTER), count)
        return put(g.at[at], g.at[at], device)

    def ring(base):
        r0 = move(base, QUARTER, right)
        l1 = move(base + QUARTER, QUARTER, left)
        r1 = move(base + QUARTER, QUARTER, right)
        l0 = move(base, QUARTER, left)
        return r0, l1, r1, l0

    def pass_on(x_of, side, copies):
        r0, l1 = copies[:2]
        r0.wait_recv()
        first = move(row(x_of, yl, side), QUARTER, right)
        l1.wait_recv()
        second = move(row(x_of, yr, side) + QUARTER, QUARTER, left)
        return first, second

    outer_half(HALF)
    over_b = move(row(xh, y, 1), HALF, across)
    outer_half(0)
    ring_a = ring(row(xh, y, 0))
    over_a = [move(row(xh, y, 0), HALF, across)]
    ring_b = ring(row(xh, y, 1))

    wait_bytes(u, zr_sem.at[1])

    def to_owner(b):
        z_of, k = b // 4, b % 4
        src = u.at[pl.ds(b * 128, 128)]
        dst = w.at[pl.ds(pl.multiple_of(c * 1024 + r * 128, 128), 128)]
        is_own = jnp.logical_and(2 * z_of + xl == r, k == 2 * xl + c)

        @pl.when(is_own)
        def _():
            pltpu.make_async_copy(src, dst, pr_sem.at[1]).start()

        @pl.when(jnp.logical_not(is_own))
        def _():
            pltpu.make_async_remote_copy(
                src_ref=src, dst_ref=dst, send_sem=ps_sem.at[1], recv_sem=pr_sem.at[1],
                device_id=(2 * z_of + xl, z * 4 + k), device_id_type=MESH,
            ).start()


    def blend(base):
        def step(i, _):
            at = pl.ds(pl.multiple_of(base + i * 16, 16), 16)
            loc[at, :] = 0.5 * loc[at, :] + 0.5 * g[at, :].astype(F32)
            return 0

        lax.fori_loop(0, HALF // 16, step, 0)

    blend(row(xh, y, 1))
    to_owner(0); to_owner(1)
    blend(row(xh, y, 0))
    to_owner(2); to_owner(3)
    on_a = pass_on(xh, 0, ring_a)
    ring_a[2].wait_recv()
    over_a.append(move(row(xh, yl, 0), HALF, across))
    ring_a[3].wait_recv()
    over_a.append(move(row(xh, yr, 0), HALF, across))
    blend(row(xh, yl, 0))
    to_owner(4); to_owner(5)
    blend(row(xh, yr, 0))
    to_owner(6); to_owner(7)
    over_b.wait_recv()
    ring_x = ring(row(far, y, 1))
    blend(row(far, y, 1))
    to_owner(8); to_owner(9)
    on_b = pass_on(xh, 1, ring_b)
    for copy in on_a:
        copy.wait_recv()
    over_a.append(move(row(xh, yo, 0), HALF, across))
    blend(row(xh, yo, 0))
    to_owner(10); to_owner(11)
    for copy in ring_b[2:]:
        copy.wait_recv()
    blend(row(xh, yl, 1))
    to_owner(12); to_owner(13)
    blend(row(xh, yr, 1))
    to_owner(14); to_owner(15)

    over_a[0].wait_recv()
    blend(row(far, y, 0))
    on_x = pass_on(far, 1, ring_x)
    for copy in on_b:
        copy.wait_recv()
    blend(row(xh, yo, 1))
    for copy in ring_x[2:]:
        copy.wait_recv()
    blend(row(far, yl, 1))
    blend(row(far, yr, 1))
    over_a[1].wait_recv()
    blend(row(far, yl, 0))
    over_a[2].wait_recv()
    blend(row(far, yr, 0))
    wait_bytes(w, pr_sem.at[1])

    def finish(i, _):
        at = pl.ds(pl.multiple_of(i * 128, 128), 128)
        clipped = factor * w[at, :].astype(F32)
        momentum = MOMENTUM_RATE * mo[at, :] + clipped
        ow[at, :] = ow[at, :] - OUTER_RATE * (clipped + MOMENTUM_RATE * momentum)
        mo[at, :] = momentum
        return 0

    lax.fori_loop(0, 16, finish, 0)

    for copy in on_x:
        copy.wait_recv()
    blend(row(far, yo, 1))
    over_a[3].wait_recv()
    blend(row(far, yo, 0))

    for copy in sent:
        copy.wait_send()
    wait_bytes(t.at[pl.ds(0, 3)], zs_sem.at[0])
    wait_bytes(u.at[pl.ds(0, 1536)], zs_sem.at[1])
    wait_bytes(u.at[pl.ds(0, 1792)], ps_sem.at[0])
    wait_bytes(u.at[pl.ds(0, 1536)], ps_sem.at[2])
    in_place = y % 2 == xl

    @pl.when(in_place)
    def _():
        wait_bytes(u.at[pl.ds(0, 1920)], ps_sem.at[1])

    @pl.when(jnp.logical_not(in_place))
    def _():
        wait_bytes(u, ps_sem.at[1])


def on_device(local_weights, anchor, outer_weights, momentum):
    _, rows, width = local_weights.shape
    owned, tile = outer_weights.shape
    whole = pl.BlockSpec(memory_space=pl.ANY)
    vmem = pltpu.VMEM
    dma = pltpu.SemaphoreType.DMA
    return pl.pallas_call(
        kernel,
        out_shape=(
            vmem((owned, tile), F32),
            vmem((owned, tile), F32),
            vmem((1, rows, width), F32),
        ),
        in_specs=[whole] * 4,
        out_specs=(pl.BlockSpec(memory_space=vmem),) * 3,
        scratch_shapes=[
            vmem((rows, width), BF16),
            vmem((rows, width), BF16),
            vmem((4 * HALF, width), BF16),
            vmem((128, width), BF16),
            vmem((256, width), BF16),
            vmem((64, width), BF16),
            vmem((128, width), BF16),
            vmem((HALF, width), BF16),
            vmem((PIECE, width), F32),
            vmem((16 * PIECE, 128), BF16),
            vmem((rows, width), BF16),
            vmem((16 * PIECE, 128), BF16),
            vmem((owned, tile), BF16),
            vmem((2, 4, 2, PIECE, 128), BF16),
            vmem((4, 2, 2, PIECE, 128), BF16),
            vmem((4, 2, 2, PIECE, 128), BF16),
            vmem((4, 2, 2, PIECE, 128), BF16),
            vmem((8, 128), F32),
            vmem((128, 128), F32),
            vmem((8, 128), F32),
            vmem((64, 128), F32),
            dma((32,)),
            dma((2,)),
            dma((64,)),
            dma((64,)),
            dma((2,)),
            dma((2,)),
            dma((3,)),
            dma((3,)),
            dma((2,)),
            dma((2,)),
        ],
        compiler_params=pltpu.CompilerParams(
            collective_id=0, has_side_effects=True, vmem_limit_bytes=36 << 20
        ),
    )(*(pltpu.with_memory_space_constraint(a, pltpu.HBM) for a in (local_weights, anchor, outer_weights, momentum)))


def solution(mesh):
    placed = (
        P("replica", "fsdp", None),
        P("fsdp", None),
        P("replica", "fsdp"),
        P("replica", "fsdp"),
    )
    return jax.shard_map(
        on_device,
        mesh=mesh,
        in_specs=placed,
        out_specs=(P("replica", "fsdp"), P("replica", "fsdp"), P("replica", "fsdp", None)),
        check_vma=False,
    )
```

```python
import jax
import jax.numpy as jnp
from jax import lax
from jax.experimental import pallas as pl
from jax.experimental.pallas import tpu as pltpu
from jax.sharding import PartitionSpec as P

MESH = pl.DeviceIdType.MESH
BF16 = jnp.bfloat16
F32 = jnp.float32

QB = 128
CLIP_RMS = 0.1
OUTER_RATE = 0.7
MOMENTUM_RATE = 0.9
LEVELS = 127.0

NR = 8
NF = 16
PIECE = 128
HALF = 64
SPLIT = 896
LOOKAHEAD = 4


def kernel(
    loc_h, anc_h, ow_h, mo_h,
    ow, mo, blended,
    anc, dq, ra, relb, finb, rela, fina, xb, tot, toth, g,
    u, vx, w, oh, v, t, obuf, part, s1, part2, s2,
    ld, iosem, ss, rs, zs_sem, zr_sem, ps_sem, pr_sem, as_sem, ar_sem,
):
    rows, width = dq.shape
    loc = blended.at[0]
    r = lax.axis_index("replica")
    f = lax.axis_index("fsdp")
    xh, y = r // 4, r % 4
    z, xl, c = f // 4, (f // 2) % 2, f % 2
    chip = r * 2 + xl
    column = z * 2 + c
    yl, yr, yo = (y + 3) % 4, (y + 1) % 4, (y + 2) % 4
    left = (xh * 4 + yl, f)
    right = (xh * 4 + yr, f)
    across = ((1 - xh) * 4 + y, f)

    def row(x_of, y_of, offset=0):
        return pl.multiple_of((4 * x_of + y_of) * PIECE + offset, HALF)

    spans = ((0, SPLIT), (SPLIT, width - SPLIT))
    cols = [pl.ds(*span) for span in spans]

    far = 1 - xh
    units = [
        (far, yo, 1), (far, yo, 0), (far, yr, 1), (far, yl, 1), (far, yr, 0), (xh, yo, 1),
        (far, yl, 0), (xh, yr, 1), (xh, yl, 1), (far, y, 0), (far, y, 1), (xh, yo, 0),
        (xh, yr, 0), (xh, yl, 0), (xh, y, 1), (xh, y, 0),
    ]
    loads = []
    for k, unit in enumerate(units):
        at, where = pl.ds(row(*unit[:2]), PIECE), cols[unit[2]]
        loads.append(
            (
                pltpu.make_async_copy(loc_h.at[0, at, where], loc.at[at, where], ld.at[2 * k]),
                pltpu.make_async_copy(anc_h.at[at, where], anc.at[at, where], ld.at[2 * k + 1]),
            )
        )
    state_in = (
        pltpu.make_async_copy(ow_h, ow, iosem.at[0]),
        pltpu.make_async_copy(mo_h, mo, iosem.at[1]),
    )

    def begin(k):
        for copy in loads[k]:
            copy.start()

    begin(0)
    for copy in state_in:
        copy.start()
    for k in range(1, LOOKAHEAD):
        begin(k)

    barrier = pltpu.get_barrier_semaphore()

    def greet(*device):
        pl.semaphore_signal(barrier, inc=1, device_id=device, device_id_type=MESH)

    def greet_chip(i, _):
        other = (chip + i) % 16
        greet(other // 2, z * 4 + (other % 2) * 2 + c)
        return 0

    lax.fori_loop(1, 16, greet_chip, 0)
    for d in range(4):
        greet(xh * 4 + (y + d) % 4, z * 4 + xl * 2 + 1 - c)
    for d in (1, 2, 3):
        for c_of in (0, 1):
            greet(r, ((z + d) % 4) * 4 + xl * 2 + c_of)

    def quantize(k):
        for copy in loads[k]:
            copy.wait()
        if k + LOOKAHEAD < len(units):
            begin(k + LOOKAHEAD)
        base = row(*units[k][:2])
        first, count = spans[units[k][2]]

        def step(i, _):
            at = pl.ds(pl.multiple_of(base + i * 32, 32), 32)
            for b in range(first, first + count, QB):
                where = pl.ds(b, QB)
                block = anc[at, where].astype(F32) - loc[at, where]
                largest = jnp.max(jnp.abs(block), axis=1, keepdims=True)
                scale = ((largest + 1e-06) / LEVELS).astype(BF16).astype(F32)
                level = jnp.floor(block / scale + 0.5)
                dq[at, where] = (level * scale).astype(BF16)
            return 0

        lax.fori_loop(0, PIECE // 32, step, 0)

    def add(dst, side, terms, count):
        dst_ref, dst_base = dst

        def read(ref, at):
            return (ref[at, cols[side]] if ref is dq else ref[at, :]).astype(F32)

        def step(i, _):
            value = None
            for ref, base in terms:
                x = read(ref, pl.ds(pl.multiple_of(base + i * 16, 16), 16))
                value = x if value is None else value + x
            dst_ref[pl.ds(pl.multiple_of(dst_base + i * 16, 16), 16), cols[side]] = value.astype(BF16)
            return 0

        lax.fori_loop(0, count // 16, step, 0)

    def wait_bytes(ref, sem):
        pltpu.make_async_copy(ref, ref, sem).wait()

    sent = []

    def put(src, dst, device):
        k = len(sent)
        copy = pltpu.make_async_remote_copy(
            src_ref=src, dst_ref=dst, send_sem=ss.at[k], recv_sem=rs.at[k],
            device_id=device, device_id_type=MESH,
        )
        copy.start()
        sent.append(copy)
        return copy

    def prepare(i, _):
        at = pl.ds(pl.multiple_of(i * 128, 128), 128)
        oh[i // 8, i % 4, (i // 4) % 2] = (
            ow[at, :] - (OUTER_RATE * MOMENTUM_RATE * MOMENTUM_RATE) * mo[at, :]
        ).astype(BF16)
        return 0

    fb = [far, xh]
    ay = [yo, yr, yl, y]
    ra_copies, rela_copies, fina_copies, xb_copies = [], [], [], []
    relb_copies, finb_copies = [[], []], [[], []]
    carry = [jnp.zeros((8, 128), F32)]

    def send(base, side, count, dst, dst_base, device):
        return put(
            dq.at[pl.ds(base, count), cols[side]], dst.at[pl.ds(dst_base, count)], device
        )

    def far_b(j):
        base = row(fb[j], yo)
        relb_copies[j] = [
            send(base, 1, HALF, relb, j * PIECE, right),
            send(base + HALF, 1, HALF, relb, j * PIECE + HALF, left),
        ]

    def near_b(j):
        into = 2 * j * PIECE
        finb_copies[j].append(send(row(fb[j], yr, HALF), 1, HALF, finb, into + HALF, right))
        finb_copies[j].append(send(row(fb[j], yl), 1, HALF, finb, into + PIECE, left))

    def relay_b(j):
        into = 2 * j * PIECE
        relb_copies[j][0].wait_recv()
        base = row(fb[j], yr)
        add((dq, base), 1, ((dq, base), (relb, j * PIECE)), HALF)
        finb_copies[j].append(send(base, 1, HALF, finb, into, right))
        relb_copies[j][1].wait_recv()
        base = row(fb[j], yl, HALF)
        add((dq, base), 1, ((dq, base), (relb, j * PIECE + HALF)), HALF)
        finb_copies[j].append(send(base, 1, HALF, finb, into + PIECE + HALF, left))

    def sum_b():
        for copy in finb_copies[0]:
            copy.wait_recv()
        base = row(far, y)
        add((dq, base), 1, ((dq, base), (finb, 0), (finb, PIECE)), PIECE)
        xb_copies.append(send(base, 1, PIECE, xb, 0, across))

    def send_a(i):
        ra_copies.append(send(row(far, ay[i]), 0, PIECE, ra, i * PIECE, across))

    def pair_a(i):
        ra_copies[i].wait_recv()
        base = row(xh, ay[i])
        add((dq, base), 0, ((dq, base), (ra, i * PIECE)), PIECE)
        if i == 0:
            rela_copies.append(send(base, 0, HALF, rela, 0, right))
            rela_copies.append(send(base + HALF, 0, HALF, rela, HALF, left))
        elif i == 1:
            fina_copies.append(send(base + HALF, 0, HALF, fina, HALF, right))
        else:
            fina_copies.append(send(base, 0, HALF, fina, PIECE, left))

    def relay_a():
        rela_copies[0].wait_recv()
        base = row(xh, yr)
        add((dq, base), 0, ((dq, base), (rela, 0)), HALF)
        fina_copies.append(send(base, 0, HALF, fina, 0, right))
        rela_copies[1].wait_recv()
        base = row(xh, yl, HALF)
        add((dq, base), 0, ((dq, base), (rela, HALF)), HALF)
        fina_copies.append(send(base, 0, HALF, fina, PIECE + HALF, left))

    def total(side, terms):
        first, count = spans[side]

        def step(i, carry):
            at = pl.ds(pl.multiple_of(i * 16, 16), 16)
            value = dq[pl.ds(pl.multiple_of(row(xh, y) + i * 16, 16), 16), cols[side]].astype(F32)
            for ref, base in terms:
                value = value + ref[pl.ds(pl.multiple_of(base + i * 16, 16), 16), :].astype(F32)
            tot[at, cols[side]] = value
            square = value * value
            for b in range(0, count, 128):
                block = (first + b) // 128
                toth[block // 4, (block // 2) % 2, block % 2, at, :] = value[:, b : b + 128].astype(BF16)
                carry = carry + square[0:8, b : b + 128] + square[8:16, b : b + 128]
            return carry

        carry[0] = lax.fori_loop(0, PIECE // 16, step, carry[0])

    def total_b():
        for copy in finb_copies[1]:
            copy.wait_recv()
        xb_copies[0].wait_recv()
        total(1, ((finb, 2 * PIECE), (finb, 3 * PIECE), (xb, 0)))

    def total_a():
        ra_copies[3].wait_recv()
        for copy in fina_copies:
            copy.wait_recv()
        total(0, ((ra, 3 * PIECE), (fina, 0), (fina, PIECE)))

    def share(src, dst, q, own, device):
        @pl.when(own)
        def _():
            pltpu.make_async_copy(src, dst, pr_sem.at[q]).start()

        @pl.when(jnp.logical_not(own))
        def _():
            pltpu.make_async_remote_copy(
                src_ref=src, dst_ref=dst, send_sem=ps_sem.at[q], recv_sem=pr_sem.at[q],
                device_id=device, device_id_type=MESH,
            ).start()

    def prepare_state():
        for copy in state_in:
            copy.wait()
        lax.fori_loop(0, 16, prepare, 0)

    def state_y(b):
        c_of, y_of = b // 4, b % 4
        share(
            oh.at[c_of, y_of], v.at[y, :, c], 0,
            jnp.logical_and(y_of == y, c_of == c), (xh * 4 + y_of, z * 4 + xl * 2 + c_of),
        )

    def state_wait_y():
        wait_bytes(v, pr_sem.at[0])

    def state_x(b):
        x_of, y_of = b // 4, b % 4
        share(
            v.at[y_of, x_of], t.at[2 * xh + y_of // 2, xl], 2,
            jnp.logical_and(x_of == xh, y_of % 2 == xl), (x_of * 4 + y, z * 4 + (y_of % 2) * 2 + c),
        )

    def along_z(src_of, dst_of, q):
        for dz in (1, 2, 3):
            z_of = (z + dz) % 4
            pltpu.make_async_remote_copy(
                src_ref=src_of(z_of), dst_ref=dst_of(z), send_sem=zs_sem.at[q], recv_sem=zr_sem.at[q],
                device_id=(r, z_of * 4 + xl * 2 + c), device_id_type=MESH,
            ).start()
        pltpu.make_async_copy(src_of(z), dst_of(z), zr_sem.at[q]).start()

    def state_z():
        wait_bytes(t, pr_sem.at[2])
        along_z(lambda z_of: t.at[z_of], lambda z_of: obuf.at[z_of], 0)

    def greeted():
        pl.semaphore_wait(barrier, 25)

    def run(steps):
        for step in steps:
            if isinstance(step, tuple):
                step[0](*step[1:])
            else:
                step()

    def quantize_each(*ks):
        for k in ks:
            quantize(k)

    def state_y_each(*bs):
        for b in bs:
            state_y(b)

    def state_x_each(*bs):
        for b in bs:
            state_x(b)

    run((
        prepare_state, (quantize, 0), greeted, (far_b, 0), (state_y_each, *range(8)),
        (quantize, 1), (send_a, 0), (quantize_each, 2, 3), (near_b, 0), (quantize, 4), (send_a, 1),
        (quantize, 5), (far_b, 1), (quantize, 6), (send_a, 2), (quantize_each, 7, 8), (near_b, 1),
        state_wait_y, (state_x_each, *range(8)), (relay_b, 0), (quantize, 9), (send_a, 3),
        (quantize_each, 10, 11), (pair_a, 0), (quantize_each, 12, 13), (relay_b, 1),
        (quantize_each, 14, 15), sum_b, state_z, (pair_a, 1), (pair_a, 2), relay_a, total_b, total_a,
    ))
    carry = carry[0]

    part[...] = carry
    s1[pl.ds(pl.multiple_of(chip * 8, 8), 8), :] = carry

    def tell_plane(i, _):
        other = (chip + i) % 16
        pltpu.make_async_remote_copy(
            src_ref=part, dst_ref=s1.at[pl.ds(pl.multiple_of(chip * 8, 8), 8)],
            send_sem=as_sem.at[0], recv_sem=ar_sem.at[0],
            device_id=(other // 2, z * 4 + (other % 2) * 2 + c), device_id_type=MESH,
        ).start()
        return 0

    lax.fori_loop(1, 16, tell_plane, 0)

    along_z(
        lambda z_of: toth.at[z_of],
        lambda z_of: u.at[z_of],
        1,
    )

    wait_bytes(s1.at[pl.ds(0, 15 * 8)], ar_sem.at[0])
    wait_bytes(s1.at[pl.ds(0, 15 * 8)], as_sem.at[0])
    in_plane = s1[0:8, :]
    for k in range(1, 16):
        in_plane = in_plane + s1[8 * k : 8 * k + 8, :]
    part2[...] = in_plane
    s2[pl.ds(pl.multiple_of(column * 8, 8), 8), :] = in_plane
    for d in range(1, 8):
        other = (column + d) % 8
        pltpu.make_async_remote_copy(
            src_ref=part2, dst_ref=s2.at[pl.ds(pl.multiple_of(column * 8, 8), 8)],
            send_sem=as_sem.at[1], recv_sem=ar_sem.at[1],
            device_id=(r, (other // 2) * 4 + xl * 2 + other % 2), device_id_type=MESH,
        ).start()
    wait_bytes(obuf, zr_sem.at[0])
    wait_bytes(s2.at[pl.ds(0, 56)], ar_sem.at[1])
    wait_bytes(s2.at[pl.ds(0, 56)], as_sem.at[1])
    everywhere = s2[0:8, :]
    for k in range(1, 8):
        everywhere = everywhere + s2[8 * k : 8 * k + 8, :]
    squares = jnp.sum(everywhere, keepdims=True)
    entries = float(rows * NF) * width
    mean = squares * (1.0 / (NR * NR * entries))
    factor = jnp.minimum(1.0, CLIP_RMS / jnp.sqrt(mean + 1e-06)) * (1.0 / NR)
    weight = (OUTER_RATE * (1.0 + MOMENTUM_RATE)) * factor

    own = row(xh, y)

    def outer_half(side):
        first, count = spans[side]

        def step(i, _):
            at = pl.ds(pl.multiple_of(i * 16, 16), 16)
            to = pl.ds(pl.multiple_of(own + i * 16, 16), 16)
            for b in range(first, first + count, 128):
                block = b // 128
                state = obuf[block // 4, (block // 2) % 2, block % 2, at, :]
                g[to, pl.ds(b, 128)] = (state.astype(F32) - weight * tot[at, pl.ds(b, 128)]).astype(BF16)
            return 0

        lax.fori_loop(0, PIECE // 16, step, 0)

    def move(base, count, side, device):
        part = g.at[pl.ds(pl.multiple_of(base, HALF), count), cols[side]]
        return put(part, part, device)

    def ring(x_of, side):
        base = row(x_of, y)
        r0 = move(base, HALF, side, right)
        l1 = move(base + HALF, HALF, side, left)
        r1 = move(base + HALF, HALF, side, right)
        l0 = move(base, HALF, side, left)
        return r0, l1, r1, l0

    def pass_on(x_of, side, copies):
        copies[0].wait_recv()
        first = move(row(x_of, yl), HALF, side, right)
        copies[1].wait_recv()
        second = move(row(x_of, yr, HALF), HALF, side, left)
        return first, second

    def value_x(x_of, x_lo):
        share(
            u.at[pl.ds(2 * x_of, 2), x_lo], vx.at[xh, xl], 1,
            jnp.logical_and(x_of == xh, x_lo == xl), (x_of * 4 + y, z * 4 + x_lo * 2 + c),
        )

    def value_y(y_of, c_of):
        share(
            vx.at[:, y_of % 2, y_of // 2, c_of], w.at[c, :, y], 3,
            jnp.logical_and(y_of == y, c_of == c), (xh * 4 + y_of, z * 4 + xl * 2 + c_of),
        )

    def blend(x_of, y_of, side):
        base = row(x_of, y_of)

        def step(i, _):
            at = pl.ds(pl.multiple_of(base + i * 32, 32), 32)
            loc[at, cols[side]] = 0.5 * loc[at, cols[side]] + 0.5 * g[at, cols[side]].astype(F32)
            return 0

        lax.fori_loop(0, PIECE // 32, step, 0)

    def finish(i, _):
        at = pl.ds(pl.multiple_of(i * 128, 128), 128)
        clipped = factor * w[i // 8, (i // 4) % 2, i % 4].astype(F32)
        momentum = MOMENTUM_RATE * mo[at, :] + clipped
        ow[at, :] = ow[at, :] - OUTER_RATE * (clipped + MOMENTUM_RATE * momentum)
        mo[at, :] = momentum
        return 0

    outer_half(1)
    over_b = move(own, PIECE, 1, across)
    outer_half(0)
    ring_a = ring(xh, 0)
    over_a = [move(own, PIECE, 0, across)]
    ring_b = ring(xh, 1)
    wait_bytes(u, zr_sem.at[1])
    for x_of in (0, 1):
        for x_lo in (0, 1):
            value_x(x_of, x_lo)
    blend(xh, y, 1)
    blend(xh, y, 0)
    on_a = pass_on(xh, 0, ring_a)
    ring_a[2].wait_recv()
    over_a.append(move(row(xh, yl), PIECE, 0, across))
    ring_a[3].wait_recv()
    over_a.append(move(row(xh, yr), PIECE, 0, across))
    blend(xh, yl, 0)
    blend(xh, yr, 0)
    over_b.wait_recv()
    ring_x = ring(far, 1)
    blend(far, y, 1)
    on_b = pass_on(xh, 1, ring_b)
    for copy in on_a:
        copy.wait_recv()
    over_a.append(move(row(xh, yo), PIECE, 0, across))
    blend(xh, yo, 0)
    wait_bytes(vx, pr_sem.at[1])
    for y_of in range(4):
        for c_of in (0, 1):
            value_y(y_of, c_of)
    for copy in ring_b[2:]:
        copy.wait_recv()
    blend(xh, yl, 1)
    blend(xh, yr, 1)
    over_a[0].wait_recv()
    blend(far, y, 0)
    on_x = pass_on(far, 1, ring_x)
    for copy in on_b:
        copy.wait_recv()
    blend(xh, yo, 1)
    for copy in ring_x[2:]:
        copy.wait_recv()
    blend(far, yl, 1)
    blend(far, yr, 1)
    over_a[1].wait_recv()
    blend(far, yl, 0)
    over_a[2].wait_recv()
    blend(far, yr, 0)
    wait_bytes(w, pr_sem.at[3])
    lax.fori_loop(0, 16, finish, 0)
    for copy in on_x:
        copy.wait_recv()
    blend(far, yo, 1)
    over_a[3].wait_recv()
    blend(far, yo, 0)

    for copy in sent:
        copy.wait_send()
    wait_bytes(t.at[pl.ds(0, 3)], zs_sem.at[0])
    wait_bytes(t.at[pl.ds(0, 3)], zs_sem.at[1])
    wait_bytes(oh.at[0, pl.ds(0, 3)], ps_sem.at[0])
    wait_bytes(oh.at[1], ps_sem.at[0])
    wait_bytes(t.at[pl.ds(0, 3)], ps_sem.at[1])
    wait_bytes(t.at[pl.ds(0, 3)], ps_sem.at[2])
    wait_bytes(oh.at[0, pl.ds(0, 3)], ps_sem.at[3])
    wait_bytes(oh.at[1], ps_sem.at[3])


def on_device(local_weights, anchor, outer_weights, momentum):
    _, rows, width = local_weights.shape
    owned, tile = outer_weights.shape
    whole = pl.BlockSpec(memory_space=pl.ANY)
    vmem = pltpu.VMEM
    dma = pltpu.SemaphoreType.DMA
    return pl.pallas_call(
        kernel,
        out_shape=(
            vmem((owned, tile), F32),
            vmem((owned, tile), F32),
            vmem((1, rows, width), F32),
        ),
        in_specs=[whole] * 4,
        out_specs=(pl.BlockSpec(memory_space=vmem),) * 3,
        scratch_shapes=[
            vmem((rows, width), BF16),
            vmem((rows, width), BF16),
            vmem((4 * PIECE, SPLIT), BF16),
            vmem((2 * PIECE, width - SPLIT), BF16),
            vmem((4 * PIECE, width - SPLIT), BF16),
            vmem((PIECE, SPLIT), BF16),
            vmem((2 * PIECE, SPLIT), BF16),
            vmem((PIECE, width - SPLIT), BF16),
            vmem((PIECE, width), F32),
            vmem((4, 2, 2, PIECE, 128), BF16),
            vmem((rows, width), BF16),
            vmem((4, 2, 2, PIECE, 128), BF16),
            vmem((2, 2, 2, 2, PIECE, 128), BF16),
            vmem((2, 2, 4, PIECE, 128), BF16),
            vmem((2, 4, 2, PIECE, 128), BF16),
            vmem((4, 2, 2, PIECE, 128), BF16),
            vmem((4, 2, 2, PIECE, 128), BF16),
            vmem((4, 2, 2, PIECE, 128), BF16),
            vmem((8, 128), F32),
            vmem((128, 128), F32),
            vmem((8, 128), F32),
            vmem((64, 128), F32),
            dma((32,)),
            dma((2,)),
            dma((64,)),
            dma((64,)),
            dma((2,)),
            dma((2,)),
            dma((4,)),
            dma((4,)),
            dma((2,)),
            dma((2,)),
        ],
        compiler_params=pltpu.CompilerParams(
            collective_id=0, has_side_effects=True, vmem_limit_bytes=36 << 20
        ),
    )(*(pltpu.with_memory_space_constraint(a, pltpu.HBM) for a in (local_weights, anchor, outer_weights, momentum)))


def solution(mesh):
    placed = (
        P("replica", "fsdp", None),
        P("fsdp", None),
        P("replica", "fsdp"),
        P("replica", "fsdp"),
    )
    return jax.shard_map(
        on_device,
        mesh=mesh,
        in_specs=placed,
        out_specs=(P("replica", "fsdp"), P("replica", "fsdp"), P("replica", "fsdp", None)),
        check_vma=False,
    )
```

```python
import jax
import jax.numpy as jnp
from jax import lax
from jax.experimental import pallas as pl
from jax.experimental.pallas import tpu as pltpu
from jax.sharding import PartitionSpec as P

MESH = pl.DeviceIdType.MESH
BF16 = jnp.bfloat16
F32 = jnp.float32

QB = 128
CLIP_RMS = 0.1
OUTER_RATE = 0.7
MOMENTUM_RATE = 0.9
LEVELS = 127.0

NR = 8
NF = 16
PIECE = 128
HALF = 64
SPLIT = 896
BACK = 896
LOOKAHEAD = 4


def kernel(
    loc_h, anc_h, ow_h, mo_h,
    ow, mo, blended,
    anc, dq, ra, relb, finb, rela, fina, xb, tot, toth, g,
    u, vx, w, oh, v, t, obuf, part, s1, part2, s2,
    ld, iosem, ss, rs, zs_sem, zr_sem, ps_sem, pr_sem, as_sem, ar_sem,
):
    rows, width = dq.shape
    loc = blended.at[0]
    r = lax.axis_index("replica")
    f = lax.axis_index("fsdp")
    xh, y = r // 4, r % 4
    z, xl, c = f // 4, (f // 2) % 2, f % 2
    chip = r * 2 + xl
    column = z * 2 + c
    yl, yr, yo = (y + 3) % 4, (y + 1) % 4, (y + 2) % 4
    left = (xh * 4 + yl, f)
    right = (xh * 4 + yr, f)
    across = ((1 - xh) * 4 + y, f)

    def row(x_of, y_of, offset=0):
        return pl.multiple_of((4 * x_of + y_of) * PIECE + offset, HALF)

    spans = ((0, SPLIT), (SPLIT, width - SPLIT))
    cols = [pl.ds(*span) for span in spans]
    back_spans = ((0, BACK), (BACK, width - BACK))
    back = [pl.ds(*span) for span in back_spans]

    far = 1 - xh
    units = [
        (far, yo, 1), (far, yo, 0), (far, yr, 1), (far, yl, 1), (far, yr, 0), (xh, yo, 1),
        (far, yl, 0), (xh, yr, 1), (xh, yl, 1), (far, y, 0), (far, y, 1), (xh, yo, 0),
        (xh, yr, 0), (xh, yl, 0), (xh, y, 1), (xh, y, 0),
    ]
    loads = []
    for k, unit in enumerate(units):
        at, where = pl.ds(row(*unit[:2]), PIECE), cols[unit[2]]
        loads.append(
            (
                pltpu.make_async_copy(loc_h.at[0, at, where], loc.at[at, where], ld.at[2 * k]),
                pltpu.make_async_copy(anc_h.at[at, where], anc.at[at, where], ld.at[2 * k + 1]),
            )
        )
    state_in = (
        pltpu.make_async_copy(ow_h, ow, iosem.at[0]),
        pltpu.make_async_copy(mo_h, mo, iosem.at[1]),
    )

    def begin(k):
        for copy in loads[k]:
            copy.start()

    begin(0)
    for copy in state_in:
        copy.start()
    for k in range(1, LOOKAHEAD):
        begin(k)

    barrier = pltpu.get_barrier_semaphore()

    def greet(*device):
        pl.semaphore_signal(barrier, inc=1, device_id=device, device_id_type=MESH)

    def greet_chip(i, _):
        other = (chip + i) % 16
        greet(other // 2, z * 4 + (other % 2) * 2 + c)
        return 0

    lax.fori_loop(1, 16, greet_chip, 0)
    for d in range(4):
        greet(xh * 4 + (y + d) % 4, z * 4 + xl * 2 + 1 - c)
    for d in (1, 2, 3):
        for c_of in (0, 1):
            greet(r, ((z + d) % 4) * 4 + xl * 2 + c_of)

    def quantize(k):
        for copy in loads[k]:
            copy.wait()
        if k + LOOKAHEAD < len(units):
            begin(k + LOOKAHEAD)
        base = row(*units[k][:2])
        first, count = spans[units[k][2]]

        def step(i, _):
            at = pl.ds(pl.multiple_of(base + i * 32, 32), 32)
            for b in range(first, first + count, QB):
                where = pl.ds(b, QB)
                block = anc[at, where].astype(F32) - loc[at, where]
                largest = jnp.max(jnp.abs(block), axis=1, keepdims=True)
                scale = ((largest + 1e-06) / LEVELS).astype(BF16).astype(F32)
                level = jnp.floor(block / scale + 0.5)
                dq[at, where] = (level * scale).astype(BF16)
            return 0

        lax.fori_loop(0, PIECE // 32, step, 0)

    def add(dst, side, terms, count):
        dst_ref, dst_base = dst

        def read(ref, at):
            return (ref[at, cols[side]] if ref is dq else ref[at, :]).astype(F32)

        def step(i, _):
            value = None
            for ref, base in terms:
                x = read(ref, pl.ds(pl.multiple_of(base + i * 16, 16), 16))
                value = x if value is None else value + x
            dst_ref[pl.ds(pl.multiple_of(dst_base + i * 16, 16), 16), cols[side]] = value.astype(BF16)
            return 0

        lax.fori_loop(0, count // 16, step, 0)

    def wait_bytes(ref, sem):
        pltpu.make_async_copy(ref, ref, sem).wait()

    sent = []

    def put(src, dst, device):
        k = len(sent)
        copy = pltpu.make_async_remote_copy(
            src_ref=src, dst_ref=dst, send_sem=ss.at[k], recv_sem=rs.at[k],
            device_id=device, device_id_type=MESH,
        )
        copy.start()
        sent.append(copy)
        return copy

    def prepare(i, _):
        at = pl.ds(pl.multiple_of(i * 128, 128), 128)
        oh[i // 8, i % 4, (i // 4) % 2] = (
            ow[at, :] - (OUTER_RATE * MOMENTUM_RATE * MOMENTUM_RATE) * mo[at, :]
        ).astype(BF16)
        return 0

    fb = [far, xh]
    ay = [yo, yr, yl, y]
    ra_copies, rela_copies, fina_copies, xb_copies = [], [], [], []
    relb_copies, finb_copies = [[], []], [[], []]
    carry = [jnp.zeros((8, 128), F32)]

    def send(base, side, count, dst, dst_base, device):
        return put(
            dq.at[pl.ds(base, count), cols[side]], dst.at[pl.ds(dst_base, count)], device
        )

    def far_b(j):
        base = row(fb[j], yo)
        relb_copies[j] = [
            send(base, 1, HALF, relb, j * PIECE, right),
            send(base + HALF, 1, HALF, relb, j * PIECE + HALF, left),
        ]

    def near_b(j):
        into = 2 * j * PIECE
        finb_copies[j].append(send(row(fb[j], yr, HALF), 1, HALF, finb, into + HALF, right))
        finb_copies[j].append(send(row(fb[j], yl), 1, HALF, finb, into + PIECE, left))

    def relay_b(j):
        into = 2 * j * PIECE
        relb_copies[j][0].wait_recv()
        base = row(fb[j], yr)
        add((dq, base), 1, ((dq, base), (relb, j * PIECE)), HALF)
        finb_copies[j].append(send(base, 1, HALF, finb, into, right))
        relb_copies[j][1].wait_recv()
        base = row(fb[j], yl, HALF)
        add((dq, base), 1, ((dq, base), (relb, j * PIECE + HALF)), HALF)
        finb_copies[j].append(send(base, 1, HALF, finb, into + PIECE + HALF, left))

    def sum_b():
        for copy in finb_copies[0]:
            copy.wait_recv()
        base = row(far, y)
        add((dq, base), 1, ((dq, base), (finb, 0), (finb, PIECE)), PIECE)
        xb_copies.append(send(base, 1, PIECE, xb, 0, across))

    def send_a(i):
        ra_copies.append(send(row(far, ay[i]), 0, PIECE, ra, i * PIECE, across))

    def pair_a(i):
        ra_copies[i].wait_recv()
        base = row(xh, ay[i])
        add((dq, base), 0, ((dq, base), (ra, i * PIECE)), PIECE)
        if i == 0:
            rela_copies.append(send(base, 0, HALF, rela, 0, right))
            rela_copies.append(send(base + HALF, 0, HALF, rela, HALF, left))
        elif i == 1:
            fina_copies.append(send(base + HALF, 0, HALF, fina, HALF, right))
        else:
            fina_copies.append(send(base, 0, HALF, fina, PIECE, left))

    def relay_a():
        rela_copies[0].wait_recv()
        base = row(xh, yr)
        add((dq, base), 0, ((dq, base), (rela, 0)), HALF)
        fina_copies.append(send(base, 0, HALF, fina, 0, right))
        rela_copies[1].wait_recv()
        base = row(xh, yl, HALF)
        add((dq, base), 0, ((dq, base), (rela, HALF)), HALF)
        fina_copies.append(send(base, 0, HALF, fina, PIECE + HALF, left))

    def total(side, terms):
        first, count = spans[side]

        def step(i, carry):
            at = pl.ds(pl.multiple_of(i * 16, 16), 16)
            value = dq[pl.ds(pl.multiple_of(row(xh, y) + i * 16, 16), 16), cols[side]].astype(F32)
            for ref, base in terms:
                value = value + ref[pl.ds(pl.multiple_of(base + i * 16, 16), 16), :].astype(F32)
            tot[at, cols[side]] = value
            square = value * value
            for b in range(0, count, 128):
                block = (first + b) // 128
                toth[block // 4, (block // 2) % 2, block % 2, at, :] = value[:, b : b + 128].astype(BF16)
                carry = carry + square[0:8, b : b + 128] + square[8:16, b : b + 128]
            return carry

        carry[0] = lax.fori_loop(0, PIECE // 16, step, carry[0])

    def total_b():
        for copy in finb_copies[1]:
            copy.wait_recv()
        xb_copies[0].wait_recv()
        total(1, ((finb, 2 * PIECE), (finb, 3 * PIECE), (xb, 0)))

    def total_a():
        ra_copies[3].wait_recv()
        for copy in fina_copies:
            copy.wait_recv()
        total(0, ((ra, 3 * PIECE), (fina, 0), (fina, PIECE)))

    def share(src, dst, q, own, device):
        @pl.when(own)
        def _():
            pltpu.make_async_copy(src, dst, pr_sem.at[q]).start()

        @pl.when(jnp.logical_not(own))
        def _():
            pltpu.make_async_remote_copy(
                src_ref=src, dst_ref=dst, send_sem=ps_sem.at[q], recv_sem=pr_sem.at[q],
                device_id=device, device_id_type=MESH,
            ).start()

    def prepare_state():
        for copy in state_in:
            copy.wait()
        lax.fori_loop(0, 16, prepare, 0)

    def state_y(b):
        c_of, y_of = b // 4, b % 4
        share(
            oh.at[c_of, y_of], v.at[y, :, c], 0,
            jnp.logical_and(y_of == y, c_of == c), (xh * 4 + y_of, z * 4 + xl * 2 + c_of),
        )

    def state_wait_y():
        wait_bytes(v, pr_sem.at[0])

    def state_x(b):
        x_of, y_of = b // 4, b % 4
        share(
            v.at[y_of, x_of], t.at[2 * xh + y_of // 2, xl], 2,
            jnp.logical_and(x_of == xh, y_of % 2 == xl), (x_of * 4 + y, z * 4 + (y_of % 2) * 2 + c),
        )

    def along_z(src_of, dst_of, q):
        for dz in (1, 2, 3):
            z_of = (z + dz) % 4
            pltpu.make_async_remote_copy(
                src_ref=src_of(z_of), dst_ref=dst_of(z), send_sem=zs_sem.at[q], recv_sem=zr_sem.at[q],
                device_id=(r, z_of * 4 + xl * 2 + c), device_id_type=MESH,
            ).start()
        pltpu.make_async_copy(src_of(z), dst_of(z), zr_sem.at[q]).start()

    def state_z():
        wait_bytes(t, pr_sem.at[2])
        along_z(lambda z_of: t.at[z_of], lambda z_of: obuf.at[z_of], 0)

    def greeted():
        pl.semaphore_wait(barrier, 25)

    def run(steps):
        for step in steps:
            if isinstance(step, tuple):
                step[0](*step[1:])
            else:
                step()

    def quantize_each(*ks):
        for k in ks:
            quantize(k)

    def state_y_each(*bs):
        for b in bs:
            state_y(b)

    def state_x_each(*bs):
        for b in bs:
            state_x(b)

    run((
        prepare_state, (quantize, 0), greeted, (far_b, 0),
        (quantize, 1), (send_a, 0), (quantize_each, 2, 3), (near_b, 0), (state_y_each, *range(8)), (quantize, 4), (send_a, 1),
        (quantize, 5), (far_b, 1), (quantize, 6), (send_a, 2), (quantize_each, 7, 8), (near_b, 1),
        state_wait_y, (state_x_each, *range(8)), (relay_b, 0), (quantize, 9), (send_a, 3),
        (quantize_each, 10, 11), (pair_a, 0), (quantize_each, 12, 13), (relay_b, 1),
        (quantize_each, 14, 15), sum_b, state_z, (pair_a, 1), (pair_a, 2), relay_a, total_b, total_a,
    ))
    carry = carry[0]

    part[...] = carry
    s1[pl.ds(pl.multiple_of(chip * 8, 8), 8), :] = carry

    def tell_chip(d):
        x_of, y_of = (2 * xh + xl + d // 4) % 4, (y + d) % 4
        pltpu.make_async_remote_copy(
            src_ref=part, dst_ref=s1.at[pl.ds(pl.multiple_of(chip * 8, 8), 8)],
            send_sem=as_sem.at[0], recv_sem=ar_sem.at[0],
            device_id=((x_of // 2) * 4 + y_of, z * 4 + (x_of % 2) * 2 + c), device_id_type=MESH,
        ).start()

    for d in (13, 14, 15, 9, 10, 11, 5, 6, 7, 12, 8, 4, 1, 2, 3):
        tell_chip(d)


    wait_bytes(s1.at[pl.ds(0, 15 * 8)], ar_sem.at[0])
    in_plane = s1[0:8, :]
    for k in range(1, 16):
        in_plane = in_plane + s1[8 * k : 8 * k + 8, :]
    part2[...] = in_plane
    s2[pl.ds(pl.multiple_of(column * 8, 8), 8), :] = in_plane
    for d in range(1, 8):
        other = (column + d) % 8
        pltpu.make_async_remote_copy(
            src_ref=part2, dst_ref=s2.at[pl.ds(pl.multiple_of(column * 8, 8), 8)],
            send_sem=as_sem.at[1], recv_sem=ar_sem.at[1],
            device_id=(r, (other // 2) * 4 + xl * 2 + other % 2), device_id_type=MESH,
        ).start()
    wait_bytes(obuf, zr_sem.at[0])
    wait_bytes(s2.at[pl.ds(0, 56)], ar_sem.at[1])
    everywhere = s2[0:8, :]
    for k in range(1, 8):
        everywhere = everywhere + s2[8 * k : 8 * k + 8, :]
    squares = jnp.sum(everywhere, keepdims=True)
    entries = float(rows * NF) * width
    mean = squares * (1.0 / (NR * NR * entries))
    factor = jnp.minimum(1.0, CLIP_RMS / jnp.sqrt(mean + 1e-06)) * (1.0 / NR)
    weight = (OUTER_RATE * (1.0 + MOMENTUM_RATE)) * factor

    own = row(xh, y)

    def outer_half(side):
        first, count = back_spans[side]

        def step(i, _):
            at = pl.ds(pl.multiple_of(i * 16, 16), 16)
            to = pl.ds(pl.multiple_of(own + i * 16, 16), 16)
            for b in range(first, first + count, 128):
                block = b // 128
                state = obuf[block // 4, (block // 2) % 2, block % 2, at, :]
                g[to, pl.ds(b, 128)] = (state.astype(F32) - weight * tot[at, pl.ds(b, 128)]).astype(BF16)
            return 0

        lax.fori_loop(0, PIECE // 16, step, 0)

    def move(base, count, side, device):
        part = g.at[pl.ds(pl.multiple_of(base, HALF), count), back[side]]
        return put(part, part, device)

    def ring(x_of, side):
        base = row(x_of, y)
        r0 = move(base, HALF, side, right)
        l1 = move(base + HALF, HALF, side, left)
        r1 = move(base + HALF, HALF, side, right)
        l0 = move(base, HALF, side, left)
        return r0, l1, r1, l0

    def pass_on(x_of, side, copies):
        copies[0].wait_recv()
        first = move(row(x_of, yl), HALF, side, right)
        copies[1].wait_recv()
        second = move(row(x_of, yr, HALF), HALF, side, left)
        return first, second

    def value_x(x_of, x_lo):
        share(
            u.at[pl.ds(2 * x_of, 2), x_lo], vx.at[xh, xl], 1,
            jnp.logical_and(x_of == xh, x_lo == xl), (x_of * 4 + y, z * 4 + x_lo * 2 + c),
        )

    def value_y(y_of, c_of):
        share(
            vx.at[:, y_of % 2, y_of // 2, c_of], w.at[c, :, y], 3,
            jnp.logical_and(y_of == y, c_of == c), (xh * 4 + y_of, z * 4 + xl * 2 + c_of),
        )

    def blend(x_of, y_of, side):
        base = row(x_of, y_of)

        def step(i, _):
            at = pl.ds(pl.multiple_of(base + i * 32, 32), 32)
            loc[at, back[side]] = 0.5 * loc[at, back[side]] + 0.5 * g[at, back[side]].astype(F32)
            return 0

        lax.fori_loop(0, PIECE // 32, step, 0)

    def finish(i, _):
        at = pl.ds(pl.multiple_of(i * 128, 128), 128)
        clipped = factor * w[i // 8, (i // 4) % 2, i % 4].astype(F32)
        momentum = MOMENTUM_RATE * mo[at, :] + clipped
        ow[at, :] = ow[at, :] - OUTER_RATE * (clipped + MOMENTUM_RATE * momentum)
        mo[at, :] = momentum
        return 0

    outer_half(1)
    over_b = move(own, PIECE, 1, across)
    outer_half(0)
    ring_a = ring(xh, 0)
    over_a = [move(own, PIECE, 0, across)]
    ring_b = ring(xh, 1)
    along_z(
        lambda z_of: toth.at[z_of],
        lambda z_of: u.at[z_of],
        1,
    )
    wait_bytes(u, zr_sem.at[1])
    for x_of in (0, 1):
        for x_lo in (0, 1):
            value_x(x_of, x_lo)
    blend(xh, y, 1)
    blend(xh, y, 0)
    on_a = pass_on(xh, 0, ring_a)
    ring_a[2].wait_recv()
    over_a.append(move(row(xh, yl), PIECE, 0, across))
    ring_a[3].wait_recv()
    over_a.append(move(row(xh, yr), PIECE, 0, across))
    blend(xh, yl, 0)
    blend(xh, yr, 0)
    over_b.wait_recv()
    ring_x = ring(far, 1)
    blend(far, y, 1)
    on_b = pass_on(xh, 1, ring_b)
    for copy in on_a:
        copy.wait_recv()
    over_a.append(move(row(xh, yo), PIECE, 0, across))
    blend(xh, yo, 0)
    wait_bytes(vx, pr_sem.at[1])
    for y_of in range(4):
        for c_of in (0, 1):
            value_y(y_of, c_of)
    for copy in ring_b[2:]:
        copy.wait_recv()
    blend(xh, yl, 1)
    blend(xh, yr, 1)
    over_a[0].wait_recv()
    blend(far, y, 0)
    on_x = pass_on(far, 1, ring_x)
    for copy in on_b:
        copy.wait_recv()
    blend(xh, yo, 1)
    for copy in ring_x[2:]:
        copy.wait_recv()
    blend(far, yl, 1)
    blend(far, yr, 1)
    over_a[1].wait_recv()
    blend(far, yl, 0)
    over_a[2].wait_recv()
    blend(far, yr, 0)
    wait_bytes(w, pr_sem.at[3])
    lax.fori_loop(0, 16, finish, 0)
    for copy in on_x:
        copy.wait_recv()
    blend(far, yo, 1)
    over_a[3].wait_recv()
    blend(far, yo, 0)
    wait_bytes(s1.at[pl.ds(0, 15 * 8)], as_sem.at[0])
    wait_bytes(s2.at[pl.ds(0, 56)], as_sem.at[1])

    for copy in sent:
        copy.wait_send()
    wait_bytes(t.at[pl.ds(0, 3)], zs_sem.at[0])
    wait_bytes(t.at[pl.ds(0, 3)], zs_sem.at[1])
    wait_bytes(oh.at[0, pl.ds(0, 3)], ps_sem.at[0])
    wait_bytes(oh.at[1], ps_sem.at[0])
    wait_bytes(t.at[pl.ds(0, 3)], ps_sem.at[1])
    wait_bytes(t.at[pl.ds(0, 3)], ps_sem.at[2])
    wait_bytes(oh.at[0, pl.ds(0, 3)], ps_sem.at[3])
    wait_bytes(oh.at[1], ps_sem.at[3])


def on_device(local_weights, anchor, outer_weights, momentum):
    _, rows, width = local_weights.shape
    owned, tile = outer_weights.shape
    whole = pl.BlockSpec(memory_space=pl.ANY)
    vmem = pltpu.VMEM
    dma = pltpu.SemaphoreType.DMA
    return pl.pallas_call(
        kernel,
        out_shape=(
            vmem((owned, tile), F32),
            vmem((owned, tile), F32),
            vmem((1, rows, width), F32),
        ),
        in_specs=[whole] * 4,
        out_specs=(pl.BlockSpec(memory_space=vmem),) * 3,
        scratch_shapes=[
            vmem((rows, width), BF16),
            vmem((rows, width), BF16),
            vmem((4 * PIECE, SPLIT), BF16),
            vmem((2 * PIECE, width - SPLIT), BF16),
            vmem((4 * PIECE, width - SPLIT), BF16),
            vmem((PIECE, SPLIT), BF16),
            vmem((2 * PIECE, SPLIT), BF16),
            vmem((PIECE, width - SPLIT), BF16),
            vmem((PIECE, width), F32),
            vmem((4, 2, 2, PIECE, 128), BF16),
            vmem((rows, width), BF16),
            vmem((4, 2, 2, PIECE, 128), BF16),
            vmem((2, 2, 2, 2, PIECE, 128), BF16),
            vmem((2, 2, 4, PIECE, 128), BF16),
            vmem((2, 4, 2, PIECE, 128), BF16),
            vmem((4, 2, 2, PIECE, 128), BF16),
            vmem((4, 2, 2, PIECE, 128), BF16),
            vmem((4, 2, 2, PIECE, 128), BF16),
            vmem((8, 128), F32),
            vmem((128, 128), F32),
            vmem((8, 128), F32),
            vmem((64, 128), F32),
            dma((32,)),
            dma((2,)),
            dma((64,)),
            dma((64,)),
            dma((2,)),
            dma((2,)),
            dma((4,)),
            dma((4,)),
            dma((2,)),
            dma((2,)),
        ],
        compiler_params=pltpu.CompilerParams(
            collective_id=0, has_side_effects=True, vmem_limit_bytes=36 << 20
        ),
    )(*(pltpu.with_memory_space_constraint(a, pltpu.HBM) for a in (local_weights, anchor, outer_weights, momentum)))


def solution(mesh):
    placed = (
        P("replica", "fsdp", None),
        P("fsdp", None),
        P("replica", "fsdp"),
        P("replica", "fsdp"),
    )
    return jax.shard_map(
        on_device,
        mesh=mesh,
        in_specs=placed,
        out_specs=(P("replica", "fsdp"), P("replica", "fsdp"), P("replica", "fsdp", None)),
        check_vma=False,
    )
```

```python
import jax
import jax.numpy as jnp
from jax import lax
from jax.experimental import pallas as pl
from jax.experimental.pallas import tpu as pltpu
from jax.sharding import PartitionSpec as P

MESH = pl.DeviceIdType.MESH
BF16 = jnp.bfloat16
F32 = jnp.float32

QB = 128
CLIP_RMS = 0.1
OUTER_RATE = 0.7
MOMENTUM_RATE = 0.9
LEVELS = 127.0

NR = 8
NF = 16
PIECE = 128
HALF = 64
SPLIT = 896
BACK = 896
LOOKAHEAD = 4


def kernel(
    loc_h, anc_h, ow_h, mo_h,
    clip_out, blended,
    anc, dq, ra, relb, finb, rela, fina, xb, tot, toth, g,
    u, vx, w, ow, mo, oh, v, t, obuf, part, s1, part2, s2,
    ld, iosem, ss, rs, zs_sem, zr_sem, ps_sem, pr_sem, as_sem, ar_sem,
):
    rows, width = dq.shape
    loc = blended.at[0]
    r = lax.axis_index("replica")
    f = lax.axis_index("fsdp")
    xh, y = r // 4, r % 4
    z, xl, c = f // 4, (f // 2) % 2, f % 2
    chip = r * 2 + xl
    column = z * 2 + c
    yl, yr, yo = (y + 3) % 4, (y + 1) % 4, (y + 2) % 4
    left = (xh * 4 + yl, f)
    right = (xh * 4 + yr, f)
    across = ((1 - xh) * 4 + y, f)

    def row(x_of, y_of, offset=0):
        return pl.multiple_of((4 * x_of + y_of) * PIECE + offset, HALF)

    spans = ((0, SPLIT), (SPLIT, width - SPLIT))
    cols = [pl.ds(*span) for span in spans]
    back_spans = ((0, BACK), (BACK, width - BACK))
    back = [pl.ds(*span) for span in back_spans]

    far = 1 - xh
    units = [
        (far, yo, 1), (far, yo, 0), (far, yr, 1), (far, yl, 1), (far, yr, 0), (xh, yo, 1),
        (far, yl, 0), (xh, yr, 1), (xh, yl, 1), (far, y, 0), (far, y, 1), (xh, yo, 0),
        (xh, yr, 0), (xh, yl, 0), (xh, y, 1), (xh, y, 0),
    ]
    loads = []
    for k, unit in enumerate(units):
        at, where = pl.ds(row(*unit[:2]), PIECE), cols[unit[2]]
        loads.append(
            (
                pltpu.make_async_copy(loc_h.at[0, at, where], loc.at[at, where], ld.at[2 * k]),
                pltpu.make_async_copy(anc_h.at[at, where], anc.at[at, where], ld.at[2 * k + 1]),
            )
        )
    state_in = (
        pltpu.make_async_copy(ow_h, ow, iosem.at[0]),
        pltpu.make_async_copy(mo_h, mo, iosem.at[1]),
    )

    def begin(k):
        for copy in loads[k]:
            copy.start()

    begin(0)
    for copy in state_in:
        copy.start()
    for k in range(1, LOOKAHEAD):
        begin(k)

    barrier = pltpu.get_barrier_semaphore()

    def greet(*device):
        pl.semaphore_signal(barrier, inc=1, device_id=device, device_id_type=MESH)

    def greet_chip(i, _):
        other = (chip + i) % 16
        greet(other // 2, z * 4 + (other % 2) * 2 + c)
        return 0

    lax.fori_loop(1, 16, greet_chip, 0)
    for d in range(4):
        greet(xh * 4 + (y + d) % 4, z * 4 + xl * 2 + 1 - c)
    for d in (1, 2, 3):
        for c_of in (0, 1):
            greet(r, ((z + d) % 4) * 4 + xl * 2 + c_of)

    def quantize(k):
        for copy in loads[k]:
            copy.wait()
        if k + LOOKAHEAD < len(units):
            begin(k + LOOKAHEAD)
        base = row(*units[k][:2])
        first, count = spans[units[k][2]]

        def step(i, _):
            at = pl.ds(pl.multiple_of(base + i * 32, 32), 32)
            for b in range(first, first + count, QB):
                where = pl.ds(b, QB)
                block = anc[at, where].astype(F32) - loc[at, where]
                largest = jnp.max(jnp.abs(block), axis=1, keepdims=True)
                scale = ((largest + 1e-06) / LEVELS).astype(BF16).astype(F32)
                level = jnp.floor(block / scale + 0.5)
                dq[at, where] = (level * scale).astype(BF16)
            return 0

        lax.fori_loop(0, PIECE // 32, step, 0)

    def add(dst, side, terms, count):
        dst_ref, dst_base = dst

        def read(ref, at):
            return (ref[at, cols[side]] if ref is dq else ref[at, :]).astype(F32)

        def step(i, _):
            value = None
            for ref, base in terms:
                x = read(ref, pl.ds(pl.multiple_of(base + i * 16, 16), 16))
                value = x if value is None else value + x
            dst_ref[pl.ds(pl.multiple_of(dst_base + i * 16, 16), 16), cols[side]] = value.astype(BF16)
            return 0

        lax.fori_loop(0, count // 16, step, 0)

    def wait_bytes(ref, sem):
        pltpu.make_async_copy(ref, ref, sem).wait()

    sent = []

    def put(src, dst, device):
        k = len(sent)
        copy = pltpu.make_async_remote_copy(
            src_ref=src, dst_ref=dst, send_sem=ss.at[k], recv_sem=rs.at[k],
            device_id=device, device_id_type=MESH,
        )
        copy.start()
        sent.append(copy)
        return copy

    def prepare(i, _):
        at = pl.ds(pl.multiple_of(i * 128, 128), 128)
        oh[i // 8, i % 4, (i // 4) % 2] = (
            ow[at, :] - (OUTER_RATE * MOMENTUM_RATE * MOMENTUM_RATE) * mo[at, :]
        ).astype(BF16)
        return 0

    fb = [far, xh]
    ay = [yo, yr, yl, y]
    ra_copies, rela_copies, fina_copies, xb_copies = [], [], [], []
    relb_copies, finb_copies = [[], []], [[], []]
    carry = [jnp.zeros((8, 128), F32)]

    def send(base, side, count, dst, dst_base, device):
        return put(
            dq.at[pl.ds(base, count), cols[side]], dst.at[pl.ds(dst_base, count)], device
        )

    def far_b(j):
        base = row(fb[j], yo)
        relb_copies[j] = [
            send(base, 1, HALF, relb, j * PIECE, right),
            send(base + HALF, 1, HALF, relb, j * PIECE + HALF, left),
        ]

    def near_b(j):
        into = 2 * j * PIECE
        finb_copies[j].append(send(row(fb[j], yr, HALF), 1, HALF, finb, into + HALF, right))
        finb_copies[j].append(send(row(fb[j], yl), 1, HALF, finb, into + PIECE, left))

    def relay_b(j):
        into = 2 * j * PIECE
        relb_copies[j][0].wait_recv()
        base = row(fb[j], yr)
        add((dq, base), 1, ((dq, base), (relb, j * PIECE)), HALF)
        finb_copies[j].append(send(base, 1, HALF, finb, into, right))
        relb_copies[j][1].wait_recv()
        base = row(fb[j], yl, HALF)
        add((dq, base), 1, ((dq, base), (relb, j * PIECE + HALF)), HALF)
        finb_copies[j].append(send(base, 1, HALF, finb, into + PIECE + HALF, left))

    def sum_b():
        for copy in finb_copies[0]:
            copy.wait_recv()
        base = row(far, y)
        add((dq, base), 1, ((dq, base), (finb, 0), (finb, PIECE)), PIECE)
        xb_copies.append(send(base, 1, PIECE, xb, 0, across))

    def send_a(i):
        ra_copies.append(send(row(far, ay[i]), 0, PIECE, ra, i * PIECE, across))

    def pair_a(i):
        ra_copies[i].wait_recv()
        base = row(xh, ay[i])
        add((dq, base), 0, ((dq, base), (ra, i * PIECE)), PIECE)
        if i == 0:
            rela_copies.append(send(base, 0, HALF, rela, 0, right))
            rela_copies.append(send(base + HALF, 0, HALF, rela, HALF, left))
        elif i == 1:
            fina_copies.append(send(base + HALF, 0, HALF, fina, HALF, right))
        else:
            fina_copies.append(send(base, 0, HALF, fina, PIECE, left))

    def relay_a():
        rela_copies[0].wait_recv()
        base = row(xh, yr)
        add((dq, base), 0, ((dq, base), (rela, 0)), HALF)
        fina_copies.append(send(base, 0, HALF, fina, 0, right))
        rela_copies[1].wait_recv()
        base = row(xh, yl, HALF)
        add((dq, base), 0, ((dq, base), (rela, HALF)), HALF)
        fina_copies.append(send(base, 0, HALF, fina, PIECE + HALF, left))

    def total(side, terms):
        first, count = spans[side]

        def step(i, carry):
            at = pl.ds(pl.multiple_of(i * 16, 16), 16)
            value = dq[pl.ds(pl.multiple_of(row(xh, y) + i * 16, 16), 16), cols[side]].astype(F32)
            for ref, base in terms:
                value = value + ref[pl.ds(pl.multiple_of(base + i * 16, 16), 16), :].astype(F32)
            tot[at, cols[side]] = value
            square = value * value
            for b in range(0, count, 128):
                block = (first + b) // 128
                toth[block // 4, (block // 2) % 2, block % 2, at, :] = value[:, b : b + 128].astype(BF16)
                carry = carry + square[0:8, b : b + 128] + square[8:16, b : b + 128]
            return carry

        carry[0] = lax.fori_loop(0, PIECE // 16, step, carry[0])

    def total_b():
        for copy in finb_copies[1]:
            copy.wait_recv()
        xb_copies[0].wait_recv()
        total(1, ((finb, 2 * PIECE), (finb, 3 * PIECE), (xb, 0)))

    def total_a():
        ra_copies[3].wait_recv()
        for copy in fina_copies:
            copy.wait_recv()
        total(0, ((ra, 3 * PIECE), (fina, 0), (fina, PIECE)))

    def share(src, dst, q, own, device):
        @pl.when(own)
        def _():
            pltpu.make_async_copy(src, dst, pr_sem.at[q]).start()

        @pl.when(jnp.logical_not(own))
        def _():
            pltpu.make_async_remote_copy(
                src_ref=src, dst_ref=dst, send_sem=ps_sem.at[q], recv_sem=pr_sem.at[q],
                device_id=device, device_id_type=MESH,
            ).start()

    def prepare_state():
        for copy in state_in:
            copy.wait()
        lax.fori_loop(0, 16, prepare, 0)

    def state_y(b):
        c_of, y_of = b // 4, b % 4
        share(
            oh.at[c_of, y_of], v.at[y, :, c], 0,
            jnp.logical_and(y_of == y, c_of == c), (xh * 4 + y_of, z * 4 + xl * 2 + c_of),
        )

    def state_wait_y():
        wait_bytes(v, pr_sem.at[0])

    def state_x(b):
        x_of, y_of = b // 4, b % 4
        share(
            v.at[y_of, x_of], t.at[2 * xh + y_of // 2, xl], 2,
            jnp.logical_and(x_of == xh, y_of % 2 == xl), (x_of * 4 + y, z * 4 + (y_of % 2) * 2 + c),
        )

    def along_z(src_of, dst_of, q):
        for dz in (1, 2, 3):
            z_of = (z + dz) % 4
            pltpu.make_async_remote_copy(
                src_ref=src_of(z_of), dst_ref=dst_of(z), send_sem=zs_sem.at[q], recv_sem=zr_sem.at[q],
                device_id=(r, z_of * 4 + xl * 2 + c), device_id_type=MESH,
            ).start()
        pltpu.make_async_copy(src_of(z), dst_of(z), zr_sem.at[q]).start()

    def state_z():
        wait_bytes(t, pr_sem.at[2])
        along_z(lambda z_of: t.at[z_of], lambda z_of: obuf.at[z_of], 0)

    def greeted():
        pl.semaphore_wait(barrier, 25)

    def run(steps):
        for step in steps:
            if isinstance(step, tuple):
                step[0](*step[1:])
            else:
                step()

    def quantize_each(*ks):
        for k in ks:
            quantize(k)

    def state_y_each(*bs):
        for b in bs:
            state_y(b)

    def state_x_each(*bs):
        for b in bs:
            state_x(b)

    run((
        prepare_state, (quantize, 0), greeted, (far_b, 0),
        (quantize, 1), (send_a, 0), (quantize_each, 2, 3), (near_b, 0), (state_y_each, *range(8)), (quantize, 4), (send_a, 1),
        (quantize, 5), (far_b, 1), (quantize, 6), (send_a, 2), (quantize_each, 7, 8), (near_b, 1),
        state_wait_y, (state_x_each, *range(8)), (relay_b, 0), (quantize, 9), (send_a, 3),
        (quantize_each, 10, 11), (pair_a, 0), (quantize_each, 12, 13), (relay_b, 1),
        (quantize_each, 14, 15), sum_b, state_z, (pair_a, 1), (pair_a, 2), relay_a, total_b, total_a,
    ))
    carry = carry[0]

    part[...] = carry
    s1[pl.ds(pl.multiple_of(chip * 8, 8), 8), :] = carry

    def tell_chip(d):
        x_of, y_of = (2 * xh + xl + d // 4) % 4, (y + d) % 4
        pltpu.make_async_remote_copy(
            src_ref=part, dst_ref=s1.at[pl.ds(pl.multiple_of(chip * 8, 8), 8)],
            send_sem=as_sem.at[0], recv_sem=ar_sem.at[0],
            device_id=((x_of // 2) * 4 + y_of, z * 4 + (x_of % 2) * 2 + c), device_id_type=MESH,
        ).start()

    for d in (13, 14, 15, 9, 10, 11, 5, 6, 7, 12, 8, 4, 1, 2, 3):
        tell_chip(d)


    wait_bytes(s1.at[pl.ds(0, 15 * 8)], ar_sem.at[0])
    in_plane = s1[0:8, :]
    for k in range(1, 16):
        in_plane = in_plane + s1[8 * k : 8 * k + 8, :]
    part2[...] = in_plane
    s2[pl.ds(pl.multiple_of(column * 8, 8), 8), :] = in_plane
    for d in range(1, 8):
        other = (column + d) % 8
        pltpu.make_async_remote_copy(
            src_ref=part2, dst_ref=s2.at[pl.ds(pl.multiple_of(column * 8, 8), 8)],
            send_sem=as_sem.at[1], recv_sem=ar_sem.at[1],
            device_id=(r, (other // 2) * 4 + xl * 2 + other % 2), device_id_type=MESH,
        ).start()
    wait_bytes(obuf, zr_sem.at[0])
    wait_bytes(s2.at[pl.ds(0, 56)], ar_sem.at[1])
    everywhere = s2[0:8, :]
    for k in range(1, 8):
        everywhere = everywhere + s2[8 * k : 8 * k + 8, :]
    squares = jnp.sum(everywhere, keepdims=True)
    entries = float(rows * NF) * width
    mean = squares * (1.0 / (NR * NR * entries))
    factor = jnp.minimum(1.0, CLIP_RMS / jnp.sqrt(mean + 1e-06)) * (1.0 / NR)
    weight = (OUTER_RATE * (1.0 + MOMENTUM_RATE)) * factor

    own = row(xh, y)

    def outer_half(side):
        first, count = back_spans[side]

        def step(i, _):
            at = pl.ds(pl.multiple_of(i * 16, 16), 16)
            to = pl.ds(pl.multiple_of(own + i * 16, 16), 16)
            for b in range(first, first + count, 128):
                block = b // 128
                state = obuf[block // 4, (block // 2) % 2, block % 2, at, :]
                g[to, pl.ds(b, 128)] = (state.astype(F32) - weight * tot[at, pl.ds(b, 128)]).astype(BF16)
            return 0

        lax.fori_loop(0, PIECE // 16, step, 0)

    def move(base, count, side, device):
        part = g.at[pl.ds(pl.multiple_of(base, HALF), count), back[side]]
        return put(part, part, device)

    def ring(x_of, side):
        base = row(x_of, y)
        r0 = move(base, HALF, side, right)
        l1 = move(base + HALF, HALF, side, left)
        r1 = move(base + HALF, HALF, side, right)
        l0 = move(base, HALF, side, left)
        return r0, l1, r1, l0

    def pass_on(x_of, side, copies):
        copies[0].wait_recv()
        first = move(row(x_of, yl), HALF, side, right)
        copies[1].wait_recv()
        second = move(row(x_of, yr, HALF), HALF, side, left)
        return first, second

    def value_x(x_of, x_lo):
        share(
            u.at[pl.ds(2 * x_of, 2), x_lo], vx.at[xh, xl], 1,
            jnp.logical_and(x_of == xh, x_lo == xl), (x_of * 4 + y, z * 4 + x_lo * 2 + c),
        )

    def value_y(y_of, c_of):
        share(
            vx.at[:, y_of % 2, y_of // 2, c_of], w.at[c, :, y], 3,
            jnp.logical_and(y_of == y, c_of == c), (xh * 4 + y_of, z * 4 + xl * 2 + c_of),
        )

    def blend(x_of, y_of, side):
        base = row(x_of, y_of)

        def step(i, _):
            at = pl.ds(pl.multiple_of(base + i * 32, 32), 32)
            loc[at, back[side]] = 0.5 * loc[at, back[side]] + 0.5 * g[at, back[side]].astype(F32)
            return 0

        lax.fori_loop(0, PIECE // 32, step, 0)

    def finish(i, _):
        at = pl.ds(pl.multiple_of(i * 128, 128), 128)
        clip_out[at, :] = factor * w[i // 8, (i // 4) % 2, i % 4].astype(F32)
        return 0

    outer_half(1)
    over_b = move(own, PIECE, 1, across)
    outer_half(0)
    ring_a = ring(xh, 0)
    over_a = [move(own, PIECE, 0, across)]
    ring_b = ring(xh, 1)
    along_z(
        lambda z_of: toth.at[z_of],
        lambda z_of: u.at[z_of],
        1,
    )
    wait_bytes(u, zr_sem.at[1])
    for x_of in (0, 1):
        for x_lo in (0, 1):
            value_x(x_of, x_lo)
    blend(xh, y, 1)
    blend(xh, y, 0)
    on_a = pass_on(xh, 0, ring_a)
    ring_a[2].wait_recv()
    over_a.append(move(row(xh, yl), PIECE, 0, across))
    ring_a[3].wait_recv()
    over_a.append(move(row(xh, yr), PIECE, 0, across))
    blend(xh, yl, 0)
    blend(xh, yr, 0)
    over_b.wait_recv()
    ring_x = ring(far, 1)
    blend(far, y, 1)
    on_b = pass_on(xh, 1, ring_b)
    for copy in on_a:
        copy.wait_recv()
    over_a.append(move(row(xh, yo), PIECE, 0, across))
    blend(xh, yo, 0)
    wait_bytes(vx, pr_sem.at[1])
    for y_of in range(4):
        for c_of in (0, 1):
            value_y(y_of, c_of)
    for copy in ring_b[2:]:
        copy.wait_recv()
    blend(xh, yl, 1)
    blend(xh, yr, 1)
    over_a[0].wait_recv()
    blend(far, y, 0)
    on_x = pass_on(far, 1, ring_x)
    for copy in on_b:
        copy.wait_recv()
    blend(xh, yo, 1)
    for copy in ring_x[2:]:
        copy.wait_recv()
    blend(far, yl, 1)
    blend(far, yr, 1)
    over_a[1].wait_recv()
    blend(far, yl, 0)
    over_a[2].wait_recv()
    blend(far, yr, 0)
    wait_bytes(w, pr_sem.at[3])
    lax.fori_loop(0, 16, finish, 0)
    for copy in on_x:
        copy.wait_recv()
    blend(far, yo, 1)
    over_a[3].wait_recv()
    blend(far, yo, 0)
    wait_bytes(s1.at[pl.ds(0, 15 * 8)], as_sem.at[0])
    wait_bytes(s2.at[pl.ds(0, 56)], as_sem.at[1])

    for copy in sent:
        copy.wait_send()
    wait_bytes(t.at[pl.ds(0, 3)], zs_sem.at[0])
    wait_bytes(t.at[pl.ds(0, 3)], zs_sem.at[1])
    wait_bytes(oh.at[0, pl.ds(0, 3)], ps_sem.at[0])
    wait_bytes(oh.at[1], ps_sem.at[0])
    wait_bytes(t.at[pl.ds(0, 3)], ps_sem.at[1])
    wait_bytes(t.at[pl.ds(0, 3)], ps_sem.at[2])
    wait_bytes(oh.at[0, pl.ds(0, 3)], ps_sem.at[3])
    wait_bytes(oh.at[1], ps_sem.at[3])


def on_device(local_weights, anchor, outer_weights, momentum):
    _, rows, width = local_weights.shape
    owned, tile = outer_weights.shape
    whole = pl.BlockSpec(memory_space=pl.ANY)
    vmem = pltpu.VMEM
    dma = pltpu.SemaphoreType.DMA
    clipped, blended = pl.pallas_call(
        kernel,
        out_shape=(
            vmem((owned, tile), F32),
            vmem((1, rows, width), F32),
        ),
        in_specs=[whole] * 4,
        out_specs=(pl.BlockSpec(memory_space=vmem),) * 2,
        scratch_shapes=[
            vmem((rows, width), BF16),
            vmem((rows, width), BF16),
            vmem((4 * PIECE, SPLIT), BF16),
            vmem((2 * PIECE, width - SPLIT), BF16),
            vmem((4 * PIECE, width - SPLIT), BF16),
            vmem((PIECE, SPLIT), BF16),
            vmem((2 * PIECE, SPLIT), BF16),
            vmem((PIECE, width - SPLIT), BF16),
            vmem((PIECE, width), F32),
            vmem((4, 2, 2, PIECE, 128), BF16),
            vmem((rows, width), BF16),
            vmem((4, 2, 2, PIECE, 128), BF16),
            vmem((2, 2, 2, 2, PIECE, 128), BF16),
            vmem((2, 2, 4, PIECE, 128), BF16),
            vmem((owned, tile), F32),
            vmem((owned, tile), F32),
            vmem((2, 4, 2, PIECE, 128), BF16),
            vmem((4, 2, 2, PIECE, 128), BF16),
            vmem((4, 2, 2, PIECE, 128), BF16),
            vmem((4, 2, 2, PIECE, 128), BF16),
            vmem((8, 128), F32),
            vmem((128, 128), F32),
            vmem((8, 128), F32),
            vmem((64, 128), F32),
            dma((32,)),
            dma((2,)),
            dma((64,)),
            dma((64,)),
            dma((2,)),
            dma((2,)),
            dma((4,)),
            dma((4,)),
            dma((2,)),
            dma((2,)),
        ],
        compiler_params=pltpu.CompilerParams(
            collective_id=0, has_side_effects=True, vmem_limit_bytes=36 << 20
        ),
    )(*(pltpu.with_memory_space_constraint(a, pltpu.HBM) for a in (local_weights, anchor, outer_weights, momentum)))
    new_momentum = MOMENTUM_RATE * momentum + clipped
    new_outer = outer_weights - OUTER_RATE * (clipped + MOMENTUM_RATE * new_momentum)
    return new_outer, new_momentum, blended


def solution(mesh):
    placed = (
        P("replica", "fsdp", None),
        P("fsdp", None),
        P("replica", "fsdp"),
        P("replica", "fsdp"),
    )
    return jax.shard_map(
        on_device,
        mesh=mesh,
        in_specs=placed,
        out_specs=(P("replica", "fsdp"), P("replica", "fsdp"), P("replica", "fsdp", None)),
        check_vma=False,
    )
```
